32 devices in a mesh: rep: 1, fsdp: 32 (over z, y, x, core).
Axes of the slice: x: 2, y: 2, z: 4, core: 2. Of those that a mesh axis runs over, the one named last changes fastest.
Arguments:
- acts: bfloat16 [1, 8192, 2048], P('rep', 'fsdp'), may hold values from -6 to 6
- grad_out: bfloat16 [1, 8192, 1024], P('rep', 'fsdp'), may hold values from -0.13258252 to 0.13258252
- inner_weight: float32 [1, 2048, 1024], P('rep', 'fsdp'), may hold values from -0.03 to 0.03
- first_moment: float32 [1, 2048, 1024], P('rep', 'fsdp'), may hold values from -6 to 6
- second_moment: float32 [1, 2048, 1024], P('rep', 'fsdp'), may hold values from 0.1 to 10
- outer_weight: float32 [2048, 1024], P(('fsdp', 'rep')), may hold values from -0.03 to 0.03
- outer_momentum: float32 [2048, 1024], P(('fsdp', 'rep')), may hold values from -0.0006 to 0.0006
Outputs:
- outer_next: float32 [2048, 1024], P(('fsdp', 'rep'))
- momentum_next: float32 [2048, 1024], P(('fsdp', 'rep'))
- weight_next: bfloat16 [2048, 1024], P('fsdp')
The draws below stay inside these ranges and needn't reach their ends.
All inputs are finite; a program needn't handle non-finite values.
Results may differ from the reference program's by a relative error of at most 0.008.
Values may be sent and summed in bfloat16 or wider, within the bound.
A program may use at most 64 MiB of HBM per device.

```python
import math
import jax
import jax.numpy as jnp
from jax import lax

D = 2048
KVW = 1024
TOK_DEV = 256
INNER_STEP = 500
REPLICAS = 1
TOKENS = 8192
N_FSDP = 32


def shared_weight(key):
    return jnp.clip(jax.random.normal(key, (D, KVW), jnp.float32), -6.0, 6.0) * (0.1 * D ** (-0.5))


def draw_outer_weight(key, part):
    common = shared_weight(key)
    return common


def draw_inner_weight(key, part):
    common = shared_weight(key)
    key = jax.random.fold_in(key, 2)
    key_common, key_own = jax.random.split(key)
    together = jnp.clip(jax.random.normal(key_common, (D, KVW), jnp.float32), -4.0, 4.0) * 0.0001
    apart = jnp.clip(jax.random.normal(key_own, (REPLICAS, D, KVW), jnp.float32), -4.0, 4.0) * 0.0003
    return common[None] + together[None] + apart


def draw_acts(key, part):
    key = jax.random.fold_in(key, 3)
    key_common, key_own = jax.random.split(key)
    shared = jax.random.normal(key_common, (TOKENS, D), jnp.float32)
    own = jax.random.normal(key_own, (REPLICAS, TOKENS, D), jnp.float32)
    mixed = 0.8944272 * shared[None] + 0.4472136 * own
    return jnp.clip(mixed, -6.0, 6.0).astype(jnp.bfloat16)


def draw_grad_out(key, part):
    key = jax.random.fold_in(key, 4)
    key_common, key_own = jax.random.split(key)
    shared = jax.random.normal(key_common, (TOKENS, KVW), jnp.float32)
    own = jax.random.normal(key_own, (REPLICAS, TOKENS, KVW), jnp.float32)
    mixed = 0.8944272 * shared[None] + 0.4472136 * own
    return (jnp.clip(mixed, -6.0, 6.0) * (2.0 * TOKENS ** (-0.5))).astype(jnp.bfloat16)


def shard_levels(rng, extent, cuts, low, largest):
    gain = 1.0
    for axis_at, parts in cuts:
        steps = jax.random.uniform(jax.random.fold_in(jax.random.fold_in(rng, 6), axis_at), (parts,), jnp.float32, low / len(cuts), largest / len(cuts))
        gain = gain * jnp.repeat(jnp.exp(steps), extent[axis_at] // parts).reshape((-1,) + (1,) * (len(extent) - 1 - axis_at))
    return gain


def centred(rng, shape, spread, most, pieces=(), held_as=jnp.bfloat16):
    drawn = spread * jax.random.normal(rng, shape, jnp.float32)
    if pieces:
        drawn = drawn * shard_levels(rng, shape, pieces, -0.22, 0.18)
    return jnp.clip(drawn, -most, most).astype(held_as)


def setup_inputs(seed: int = 0) -> dict:
    splits = jax.random.split(jax.random.key(seed), 8)
    return {
        "acts": draw_acts(jax.random.fold_in(splits[7], 71), 0),
        "grad_out": draw_grad_out(jax.random.fold_in(splits[7], 71), 0),
        "inner_weight": draw_inner_weight(jax.random.fold_in(splits[7], 71), 0),
        "first_moment": centred(splits[3], (REPLICAS, D, KVW), 1.0, 6.0, ((1, 32),), jnp.float32),
        "second_moment": jnp.clip(jnp.exp(math.log(10.0) - 4.6051702 * jax.random.uniform(splits[4], (REPLICAS, D, KVW), jnp.float32) ** shard_levels(splits[4], (REPLICAS, D, KVW), ((1, 32),), -0.2, 0.2)), 0.1, 10.0),
        "outer_weight": draw_outer_weight(jax.random.fold_in(splits[7], 71), 0),
        "outer_momentum": centred(splits[6], (D, KVW), 0.0001, 0.0006, ((0, 32),), jnp.float32),
    }


def replica_step(acts, grad_out, inner_weight, first_moment, second_moment):
    blocks = acts.reshape(N_FSDP, TOK_DEV, D)
    cotangents = grad_out.reshape(N_FSDP, TOK_DEV, KVW)

    def add_block(total, pair):
        partial_sum = jnp.dot(pair[0].T, pair[1], preferred_element_type=jnp.float32).astype(jnp.bfloat16)
        return (total + partial_sum.astype(jnp.float32), None)
    grad, unused = lax.scan(add_block, jnp.zeros((D, KVW), jnp.float32), (blocks, cotangents))
    first = 0.9 * first_moment + 0.1 * grad
    second = 0.95 * second_moment + 0.05 * grad * grad
    first_hat = first / (1.0 - 0.9 ** INNER_STEP)
    second_hat = second / (1.0 - 0.95 ** INNER_STEP)
    updated = inner_weight * (1.0 - 0.0004 * 0.1) - 0.0004 * first_hat / (jnp.sqrt(second_hat) + 1e-08)
    return updated

def reference(acts, grad_out, inner_weight, first_moment, second_moment, outer_weight, outer_momentum):

    def add_replica(total, items):
        inner_new = replica_step(*items)
        return (total + inner_new, None)
    summed, unused = lax.scan(add_replica, jnp.zeros((D, KVW), jnp.float32), (acts, grad_out, inner_weight, first_moment, second_moment))
    pseudo = outer_weight - summed / REPLICAS
    momentum_next = 0.9 * outer_momentum + pseudo
    outer_next = outer_weight - 0.7 * (pseudo + 0.9 * momentum_next)
    return (outer_next, momentum_next, outer_next.astype(jnp.bfloat16))
```

```python
import functools

import jax
import jax.numpy as jnp
from jax import lax
from jax.experimental import pallas as pl
from jax.experimental.pallas import tpu as pltpu
from jax.sharding import PartitionSpec as P

INNER_STEP = 500
LANES = 128
WIDE = 2 * LANES
MESH = pl.DeviceIdType.MESH

ORDERS = (
    (1, 2, 3, 4),
    (2, 1, 3, 4),
    (3, 1, 2, 4),
    (3, 2, 1, 4),
    (1, 2, 3, 4),
    (2, 1, 3, 4),
    (1, 2, 3, 4),
    (2, 1, 3, 4),
)


def kernel(
    acts_hbm, cot_hbm, grad_ref,
    acts, cot, cot_peer, lhs, lhs_peer, part, in0, in1, in2, in3,
    load_sem, cot_send, cot_recv, lhs_send, lhs_recv, send_sem, recv_sem,
):
    me = lax.axis_index("fsdp")
    bit = [lax.rem(me // (1 << b), 2) for b in range(5)]
    peer = [me + (1 - 2 * bit[b]) * (1 << b) for b in range(5)]
    core = bit[0]
    tokens, width = cot.shape
    rows, tiles = grad_ref.shape[0], acts.shape[1] // LANES
    groups = 4
    group_rows = lhs.shape[1] // groups
    pieces, chunks = width // WIDE, width // LANES
    incoming = (in0, in1, in2, in3)

    load_acts = pltpu.make_async_copy(acts_hbm, acts, load_sem.at[0])
    load_acts.start()
    load_cot = pltpu.make_async_copy(cot_hbm, cot, load_sem.at[1])
    load_cot.start()
    barrier = pltpu.get_barrier_semaphore()
    for b in range(5):
        pl.semaphore_signal(barrier, inc=1, device_id={"fsdp": peer[b]}, device_id_type=MESH)

    def to_core(src, dst, send, recv):
        return pltpu.make_async_remote_copy(
            src_ref=src, dst_ref=dst, send_sem=send, recv_sem=recv,
            device_id={"fsdp": peer[0]}, device_id_type=MESH,
        )

    def cot_copy(j):
        cut = pl.ds(j * WIDE, WIDE)
        return to_core(cot_hbm.at[:, cut], cot_peer.at[:, cut], cot_send.at[j], cot_recv.at[j])

    def lhs_copy(g):
        cut = pl.ds(g * group_rows, group_rows)
        return to_core(lhs.at[1 - core, cut], lhs_peer.at[cut], lhs_send.at[g], lhs_recv.at[g])

    load_acts.wait()
    for t in range(tiles):
        turned = acts[:, t * LANES:(t + 1) * LANES].T
        lhs[0, t * rows:(t + 1) * rows, :] = turned[:rows]
        lhs[1, t * rows:(t + 1) * rows, :] = turned[rows:]
    pl.semaphore_wait(barrier, 5)
    cot_copy(0).start()
    for g in range(groups):
        lhs_copy(g).start()
    for j in range(1, pieces):
        cot_copy(j).start()

    def exchange(c, s):
        order = ORDERS[c % len(ORDERS)]
        kept = tuple(bit[b] for b in order[:s])
        return pltpu.make_async_remote_copy(
            src_ref=part.at[(c, *kept, 1 - bit[order[s]])],
            dst_ref=incoming[s].at[c],
            send_sem=send_sem.at[c, s],
            recv_sem=recv_sem.at[c, s],
            device_id={"fsdp": peer[order[s]]},
            device_id_type=MESH,
        )

    load_cot.wait()
    for j in range(pieces):
        cut = slice(j * WIDE, (j + 1) * WIDE)
        cot_copy(j).wait_recv()
        for g in range(groups):
            if j == 0:
                lhs_copy(g).wait_recv()
            block = slice(g * group_rows, (g + 1) * group_rows)
            product = jnp.dot(lhs[core, block, :], cot[:, cut], preferred_element_type=jnp.float32)
            product += jnp.dot(lhs_peer[block, :], cot_peer[:, cut], preferred_element_type=jnp.float32)
            product = product.astype(jnp.bfloat16)
            for k in range(group_rows // rows):
                t = g * (group_rows // rows) + k
                for h in range(2):
                    c = 2 * j + h
                    where = tuple((t >> (b - 1)) & 1 for b in ORDERS[c % len(ORDERS)])
                    part[(c, *where)] = product[k * rows:(k + 1) * rows, h * LANES:(h + 1) * LANES]
        exchange(2 * j, 0).start()
        exchange(2 * j + 1, 0).start()

    for s in range(4):
        for c in range(chunks):
            order = ORDERS[c % len(ORDERS)]
            exchange(c, s).wait_recv()
            kept = (c, *(bit[b] for b in order[: s + 1]))
            total = part[kept].astype(jnp.float32) + incoming[s][c].astype(jnp.float32)
            if s < 3:
                part[kept] = total.astype(jnp.bfloat16)
                exchange(c, s + 1).start()
            else:
                grad_ref[:, c * LANES:(c + 1) * LANES] = total
    for j in range(pieces):
        cot_copy(j).wait_send()
    for g in range(groups):
        lhs_copy(g).wait_send()
    for s in range(4):
        for c in range(chunks):
            exchange(c, s).wait_send()


def gradient(tokens, cotangent, devices):
    count, depth = tokens.shape
    width = cotangent.shape[1]
    rows, half, chunks = depth // devices, depth // 2, width // LANES
    bf16 = jnp.bfloat16
    return pl.pallas_call(
        kernel,
        out_shape=jax.ShapeDtypeStruct((rows, width), jnp.float32),
        in_specs=[pl.BlockSpec(memory_space=pl.ANY)] * 2,
        out_specs=pl.BlockSpec(memory_space=pltpu.VMEM),
        scratch_shapes=[
            pltpu.VMEM((count, depth), bf16),
            pltpu.VMEM((count, width), bf16),
            pltpu.VMEM((count, width), bf16),
            pltpu.VMEM((2, half, count), bf16),
            pltpu.VMEM((half, count), bf16),
            pltpu.VMEM((chunks, 2, 2, 2, 2, rows, LANES), bf16),
            pltpu.VMEM((chunks, 2, 2, 2, rows, LANES), bf16),
            pltpu.VMEM((chunks, 2, 2, rows, LANES), bf16),
            pltpu.VMEM((chunks, 2, rows, LANES), bf16),
            pltpu.VMEM((chunks, rows, LANES), bf16),
            pltpu.SemaphoreType.DMA((2,)),
            pltpu.SemaphoreType.DMA((width // WIDE,)),
            pltpu.SemaphoreType.DMA((width // WIDE,)),
            pltpu.SemaphoreType.DMA((4,)),
            pltpu.SemaphoreType.DMA((4,)),
            pltpu.SemaphoreType.DMA((chunks, 4)),
            pltpu.SemaphoreType.DMA((chunks, 4)),
        ],
        compiler_params=pltpu.CompilerParams(
            collective_id=0, has_side_effects=True, vmem_limit_bytes=48 * 1024 * 1024
        ),
        cost_estimate=pl.CostEstimate(
            flops=2 * count * depth * width,
            bytes_accessed=2 * count * (depth + width) + 4 * rows * width,
            transcendentals=0,
        ),
    )(tokens, cotangent)


def shards(devices, acts, grad_out, inner_weight, first_moment, second_moment, outer_weight, outer_momentum):
    grad = gradient(acts[0], grad_out[0], devices)
    first = 0.9 * first_moment[0] + 0.1 * grad
    second = 0.95 * second_moment[0] + 0.05 * grad * grad
    first_hat = first / (1.0 - 0.9**INNER_STEP)
    second_hat = second / (1.0 - 0.95**INNER_STEP)
    inner_new = inner_weight[0] * (1.0 - 0.0004 * 0.1) - 0.0004 * first_hat / (
        jnp.sqrt(second_hat) + 1e-08
    )
    replicas = lax.axis_size("rep")
    if replicas > 1:
        inner_new = lax.psum_scatter(inner_new, "rep", scatter_dimension=0, tiled=True) / replicas
    pseudo = outer_weight - inner_new
    momentum_next = 0.9 * outer_momentum + pseudo
    outer_next = outer_weight - 0.7 * (pseudo + 0.9 * momentum_next)
    weight_next = outer_next.astype(jnp.bfloat16)
    if replicas > 1:
        weight_next = lax.all_gather(weight_next, "rep", axis=0, tiled=True)
    return (outer_next, momentum_next, weight_next)


def solution(mesh):
    placed = (
        P("rep", "fsdp", None),
        P("rep", "fsdp", None),
        P("rep", "fsdp", None),
        P("rep", "fsdp", None),
        P("rep", "fsdp", None),
        P(("fsdp", "rep"), None),
        P(("fsdp", "rep"), None),
    )
    return jax.shard_map(
        functools.partial(shards, mesh.shape["fsdp"]),
        mesh=mesh,
        in_specs=placed,
        out_specs=(P(("fsdp", "rep"), None), P(("fsdp", "rep"), None), P("fsdp", None)),
        check_vma=False,
    )
```

```python
import functools

import jax
import jax.numpy as jnp
from jax import lax
from jax.experimental import pallas as pl
from jax.experimental.pallas import tpu as pltpu
from jax.sharding import PartitionSpec as P

INNER_STEP = 500
LANES = 128
WIDE = 2 * LANES
MESH = pl.DeviceIdType.MESH

TALL = (
    (1, 3, 2, 4),
    (2, 3, 1, 4),
    (3, 1, 2, 4),
    (3, 2, 1, 4),
    (1, 2, 4, 3),
    (2, 1, 4, 3),
    (1, 4, 2, 3),
    (2, 4, 1, 3),
)
SHORT = (
    (4, 1, 2, 3),
    (4, 2, 1, 3),
    (1, 2, 3, 4),
    (2, 1, 3, 4),
)


def kernel(
    acts_hbm, cot_hbm, grad_ref,
    acts, cot, cot_peer, lhs, lhs_peer,
    tall, tall0, tall1, tall2, tall3, short, short0, short1, short2, short3,
    load_sem, cot_send, cot_recv, lhs_send, lhs_recv,
    tall_send, tall_recv, short_send, short_recv,
):
    me = lax.axis_index("fsdp")
    bit = [lax.rem(me // (1 << b), 2) for b in range(5)]
    peer = [me + (1 - 2 * bit[b]) * (1 << b) for b in range(5)]
    core = bit[0]
    tokens, width = cot.shape
    rows, tiles = grad_ref.shape[0], acts.shape[1] // LANES
    groups = 4
    group_rows = lhs.shape[1] // groups
    pieces = width // WIDE
    quarter = rows // 4
    kinds = (
        (TALL, tall, (tall0, tall1, tall2, tall3), tall_send, tall_recv),
        (SHORT, short, (short0, short1, short2, short3), short_send, short_recv),
    )

    span = acts.shape[1] // groups

    def acts_copy(g):
        cut = pl.ds(g * span, span)
        return pltpu.make_async_copy(acts_hbm.at[:, cut], acts.at[:, cut], load_sem.at[g])

    for g in range(groups):
        acts_copy(g).start()
    load_cot = pltpu.make_async_copy(cot_hbm, cot, load_sem.at[groups])
    load_cot.start()
    barrier = pltpu.get_barrier_semaphore()
    for b in range(5):
        pl.semaphore_signal(barrier, inc=1, device_id={"fsdp": peer[b]}, device_id_type=MESH)

    def to_core(src, dst, send, recv):
        return pltpu.make_async_remote_copy(
            src_ref=src, dst_ref=dst, send_sem=send, recv_sem=recv,
            device_id={"fsdp": peer[0]}, device_id_type=MESH,
        )

    def cot_copy(j):
        cut = pl.ds(j * WIDE, WIDE)
        return to_core(cot_hbm.at[:, cut], cot_peer.at[:, cut], cot_send.at[j], cot_recv.at[j])

    def lhs_copy(g):
        cut = pl.ds(g * group_rows, group_rows)
        return to_core(lhs.at[1 - core, cut], lhs_peer.at[cut], lhs_send.at[g], lhs_recv.at[g])

    for t in range(tiles):
        if t % (tiles // groups) == 0:
            acts_copy(t // (tiles // groups)).wait()
        turned = acts[:, t * LANES:(t + 1) * LANES].T
        lhs[0, t * rows:(t + 1) * rows, :] = turned[:rows]
        lhs[1, t * rows:(t + 1) * rows, :] = turned[rows:]
    pl.semaphore_wait(barrier, 5)
    cot_copy(0).start()
    for g in range(groups):
        lhs_copy(g).start()
    for j in range(1, pieces):
        cot_copy(j).start()

    def exchange(kind, c, s):
        orders, part, incoming, send, recv = kinds[kind]
        order = orders[c % len(orders)]
        kept = tuple(bit[b] for b in order[:s])
        return pltpu.make_async_remote_copy(
            src_ref=part.at[(c, *kept, 1 - bit[order[s]])],
            dst_ref=incoming[s].at[c],
            send_sem=send.at[c, s],
            recv_sem=recv.at[c, s],
            device_id={"fsdp": peer[order[s]]},
            device_id_type=MESH,
        )

    def place(kind, c, t):
        orders = kinds[kind][0]
        return (c, *((t >> (b - 1)) & 1 for b in orders[c % len(orders)]))

    load_cot.wait()
    for j in range(pieces):
        cut = slice(j * WIDE, (j + 1) * WIDE)
        cot_copy(j).wait_recv()
        for g in range(groups):
            if j == 0:
                lhs_copy(g).wait_recv()
            own = slice(g * group_rows, (g + 1) * group_rows)
            product = jnp.dot(lhs[core, own, :], cot[:, cut], preferred_element_type=jnp.float32)
            product += jnp.dot(lhs_peer[own, :], cot_peer[:, cut], preferred_element_type=jnp.float32)
            product = product.astype(jnp.bfloat16)
            for k in range(group_rows // rows):
                t = g * (group_rows // rows) + k
                for h in range(2):
                    c = 2 * j + h
                    block = product[k * rows:(k + 1) * rows, h * LANES:(h + 1) * LANES]
                    tall[place(0, c, t)] = block[: 3 * quarter]
                    short[(*place(1, j, t), pl.ds(h * quarter, quarter))] = block[3 * quarter:]
        for kind, c in ((0, 2 * j), (0, 2 * j + 1), (1, j)):
            exchange(kind, c, 0).start()

    every = [item for j in range(pieces) for item in ((0, 2 * j), (0, 2 * j + 1), (1, j))]
    for s in range(4):
        for kind, c in every:
            orders, part, incoming = kinds[kind][:3]
            order = orders[c % len(orders)]
            exchange(kind, c, s).wait_recv()
            kept = (c, *(bit[b] for b in order[: s + 1]))
            total = part[kept].astype(jnp.float32) + incoming[s][c].astype(jnp.float32)
            if s < 3:
                part[kept] = total.astype(jnp.bfloat16)
                exchange(kind, c, s + 1).start()
            elif kind == 0:
                grad_ref[: 3 * quarter, c * LANES:(c + 1) * LANES] = total
            else:
                for h in range(2):
                    strip = slice((2 * c + h) * LANES, (2 * c + h + 1) * LANES)
                    grad_ref[3 * quarter:, strip] = total[h * quarter:(h + 1) * quarter]
    for j in range(pieces):
        cot_copy(j).wait_send()
    for g in range(groups):
        lhs_copy(g).wait_send()
    for s in range(4):
        for kind, c in every:
            exchange(kind, c, s).wait_send()


def gradient(tokens, cotangent, devices):
    count, depth = tokens.shape
    width = cotangent.shape[1]
    rows, half, chunks = depth // devices, depth // 2, width // LANES
    bf16 = jnp.bfloat16
    return pl.pallas_call(
        kernel,
        out_shape=jax.ShapeDtypeStruct((rows, width), jnp.float32),
        in_specs=[pl.BlockSpec(memory_space=pltpu.HBM)] * 2,
        out_specs=pl.BlockSpec(memory_space=pltpu.VMEM),
        scratch_shapes=[
            pltpu.VMEM((count, depth), bf16),
            pltpu.VMEM((count, width), bf16),
            pltpu.VMEM((count, width), bf16),
            pltpu.VMEM((2, half, count), bf16),
            pltpu.VMEM((half, count), bf16),
            *[pltpu.VMEM((chunks, *[2] * k, 3 * rows // 4, LANES), bf16) for k in (4, 3, 2, 1, 0)],
            *[pltpu.VMEM((chunks // 2, *[2] * k, rows // 2, LANES), bf16) for k in (4, 3, 2, 1, 0)],
            pltpu.SemaphoreType.DMA((5,)),
            pltpu.SemaphoreType.DMA((width // WIDE,)),
            pltpu.SemaphoreType.DMA((width // WIDE,)),
            pltpu.SemaphoreType.DMA((4,)),
            pltpu.SemaphoreType.DMA((4,)),
            pltpu.SemaphoreType.DMA((chunks, 4)),
            pltpu.SemaphoreType.DMA((chunks, 4)),
            pltpu.SemaphoreType.DMA((chunks // 2, 4)),
            pltpu.SemaphoreType.DMA((chunks // 2, 4)),
        ],
        compiler_params=pltpu.CompilerParams(
            collective_id=0, has_side_effects=True, vmem_limit_bytes=62 * 1024 * 1024
        ),
        cost_estimate=pl.CostEstimate(
            flops=2 * count * depth * width,
            bytes_accessed=2 * count * (depth + width) + 4 * rows * width,
            transcendentals=0,
        ),
    )(tokens, cotangent)


def shards(devices, acts, grad_out, inner_weight, first_moment, second_moment, outer_weight, outer_momentum):
    grad = gradient(acts[0], grad_out[0], devices)
    first = 0.9 * first_moment[0] + 0.1 * grad
    second = 0.95 * second_moment[0] + 0.05 * grad * grad
    first_hat = first / (1.0 - 0.9**INNER_STEP)
    second_hat = second / (1.0 - 0.95**INNER_STEP)
    inner_new = inner_weight[0] * (1.0 - 0.0004 * 0.1) - 0.0004 * first_hat / (
        jnp.sqrt(second_hat) + 1e-08
    )
    replicas = lax.axis_size("rep")
    if replicas > 1:
        inner_new = lax.psum_scatter(inner_new, "rep", scatter_dimension=0, tiled=True) / replicas
    pseudo = outer_weight - inner_new
    momentum_next = 0.9 * outer_momentum + pseudo
    outer_next = outer_weight - 0.7 * (pseudo + 0.9 * momentum_next)
    weight_next = outer_next.astype(jnp.bfloat16)
    if replicas > 1:
        weight_next = lax.all_gather(weight_next, "rep", axis=0, tiled=True)
    return (outer_next, momentum_next, weight_next)


def solution(mesh):
    placed = (
        P("rep", "fsdp", None),
        P("rep", "fsdp", None),
        P("rep", "fsdp", None),
        P("rep", "fsdp", None),
        P("rep", "fsdp", None),
        P(("fsdp", "rep"), None),
        P(("fsdp", "rep"), None),
    )
    return jax.shard_map(
        functools.partial(shards, mesh.shape["fsdp"]),
        mesh=mesh,
        in_specs=placed,
        out_specs=(P(("fsdp", "rep"), None), P(("fsdp", "rep"), None), P("fsdp", None)),
        check_vma=False,
    )
```

```python
import functools

import jax
import jax.numpy as jnp
from jax import lax
from jax.experimental import pallas as pl
from jax.experimental.pallas import tpu as pltpu
from jax.sharding import PartitionSpec as P

INNER_STEP = 500
LANES = 128
WIDE = 2 * LANES
MESH = pl.DeviceIdType.MESH

TALL = (
    (1, 3, 2, 4),
    (2, 3, 1, 4),
    (3, 1, 2, 4),
    (1, 2, 4, 3),
    (3, 2, 1, 4),
    (2, 1, 4, 3),
    (1, 4, 2, 3),
    (2, 4, 1, 3),
)
SHORT = (
    (4, 1, 2, 3),
    (2, 1, 3, 4),
    (4, 2, 1, 3),
    (1, 2, 3, 4),
)
LEAD = ((0, 0), (0, 1), (0, 2), (1, 1), (1, 0), (0, 3))
FOLLOW = ((0, 6), (0, 5), (0, 4), (0, 7), (1, 2), (1, 3))
ROUNDS = ((LEAD, 0), (LEAD, 1), (FOLLOW, 0), (LEAD, 2), (FOLLOW, 1), (LEAD, 3), (FOLLOW, 2), (FOLLOW, 3))


def kernel(
    acts_hbm, cot_hbm, grad_ref,
    acts, cot, cot_peer, lhs, lhs_peer,
    tall, tall0, tall1, tall2, tall3, short, short0, short1, short2, short3,
    load_sem, cot_send, cot_recv, lhs_send, lhs_recv,
    tall_send, tall_recv, short_send, short_recv,
):
    me = lax.axis_index("fsdp")
    bit = [lax.rem(me // (1 << b), 2) for b in range(5)]
    peer = [me + (1 - 2 * bit[b]) * (1 << b) for b in range(5)]
    core = bit[0]
    tokens, width = cot.shape
    rows, tiles = grad_ref.shape[0], acts.shape[1] // LANES
    groups = 4
    group_rows = lhs.shape[1] // groups
    pieces = width // WIDE
    quarter = rows // 4
    kinds = (
        (TALL, tall, (tall0, tall1, tall2, tall3), tall_send, tall_recv),
        (SHORT, short, (short0, short1, short2, short3), short_send, short_recv),
    )

    span = acts.shape[1] // groups

    def acts_copy(g):
        cut = pl.ds(g * span, span)
        return pltpu.make_async_copy(acts_hbm.at[:, cut], acts.at[:, cut], load_sem.at[g])

    for g in range(groups):
        acts_copy(g).start()
    load_cot = pltpu.make_async_copy(cot_hbm, cot, load_sem.at[groups])
    load_cot.start()
    barrier = pltpu.get_barrier_semaphore()
    for b in range(5):
        pl.semaphore_signal(barrier, inc=1, device_id={"fsdp": peer[b]}, device_id_type=MESH)

    def to_core(src, dst, send, recv):
        return pltpu.make_async_remote_copy(
            src_ref=src, dst_ref=dst, send_sem=send, recv_sem=recv,
            device_id={"fsdp": peer[0]}, device_id_type=MESH,
        )

    def cot_copy(j):
        cut = pl.ds(j * WIDE, WIDE)
        return to_core(cot_hbm.at[:, cut], cot_peer.at[:, cut], cot_send.at[j], cot_recv.at[j])

    def lhs_copy(g):
        cut = pl.ds(g * group_rows, group_rows)
        return to_core(lhs.at[1 - core, cut], lhs_peer.at[cut], lhs_send.at[g], lhs_recv.at[g])

    for t in range(tiles):
        if t % (tiles // groups) == 0:
            acts_copy(t // (tiles // groups)).wait()
        turned = acts[:, t * LANES:(t + 1) * LANES].T
        lhs[0, t * rows:(t + 1) * rows, :] = turned[:rows]
        lhs[1, t * rows:(t + 1) * rows, :] = turned[rows:]
    pl.semaphore_wait(barrier, 5)
    cot_copy(0).start()
    for g in range(groups):
        lhs_copy(g).start()
    for j in range(1, pieces):
        cot_copy(j).start()

    def exchange(kind, c, s):
        orders, part, incoming, send, recv = kinds[kind]
        order = orders[c % len(orders)]
        kept = tuple(bit[b] for b in order[:s])
        return pltpu.make_async_remote_copy(
            src_ref=part.at[(c, *kept, 1 - bit[order[s]])],
            dst_ref=incoming[s].at[c],
            send_sem=send.at[c, s],
            recv_sem=recv.at[c, s],
            device_id={"fsdp": peer[order[s]]},
            device_id_type=MESH,
        )

    def place(kind, c, t):
        orders = kinds[kind][0]
        return (c, *((t >> (b - 1)) & 1 for b in orders[c % len(orders)]))

    def finish(kind, c, s):
        orders, part, incoming = kinds[kind][:3]
        order = orders[c % len(orders)]
        kept = (c, *(bit[b] for b in order[: s + 1]))
        total = part[kept].astype(jnp.float32) + incoming[s][c].astype(jnp.float32)
        if s < 3:
            part[kept] = total.astype(jnp.bfloat16)
            exchange(kind, c, s + 1).start()
        elif kind == 0:
            grad_ref[: 3 * quarter, c * LANES:(c + 1) * LANES] = total
        else:
            for h in range(2):
                strip = slice((2 * c + h) * LANES, (2 * c + h + 1) * LANES)
                grad_ref[3 * quarter:, strip] = total[h * quarter:(h + 1) * quarter]

    def multiply(left, right):
        return jnp.dot(left, right, preferred_element_type=jnp.float32)

    load_cot.wait()
    for j in range(pieces):
        cut = slice(j * WIDE, (j + 1) * WIDE)
        block = [slice(g * group_rows, (g + 1) * group_rows) for g in range(groups)]
        if j == 0:
            ours = [multiply(lhs[core, block[g], :], cot[:, cut]) for g in range(groups)]
        cot_copy(j).wait_recv()
        for g in range(groups):
            if j == 0:
                lhs_copy(g).wait_recv()
                product = ours[g]
            else:
                product = multiply(lhs[core, block[g], :], cot[:, cut])
            product += multiply(lhs_peer[block[g], :], cot_peer[:, cut])
            product = product.astype(jnp.bfloat16)
            for k in range(group_rows // rows):
                t = g * (group_rows // rows) + k
                for h in range(2):
                    c = 2 * j + h
                    cell = product[k * rows:(k + 1) * rows, h * LANES:(h + 1) * LANES]
                    tall[place(0, c, t)] = cell[: 3 * quarter]
                    short[(*place(1, j, t), pl.ds(h * quarter, quarter))] = cell[3 * quarter:]
        for kind, c in ((0, 2 * j), (0, 2 * j + 1), (1, j)):
            if (kind, c) in LEAD:
                exchange(kind, c, 0).start()

    for members, s in ROUNDS:
        for (kind, c), follower in zip(members, FOLLOW):
            exchange(kind, c, s).wait_recv()
            if members is LEAD and s == 0:
                exchange(*follower, 0).start()
            finish(kind, c, s)
    for j in range(pieces):
        cot_copy(j).wait_send()
    for g in range(groups):
        lhs_copy(g).wait_send()
    for s in range(4):
        for kind, c in LEAD + FOLLOW:
            exchange(kind, c, s).wait_send()


def gradient(tokens, cotangent, devices):
    count, depth = tokens.shape
    width = cotangent.shape[1]
    rows, half, chunks = depth // devices, depth // 2, width // LANES
    bf16 = jnp.bfloat16
    return pl.pallas_call(
        kernel,
        out_shape=jax.ShapeDtypeStruct((rows, width), jnp.float32),
        in_specs=[pl.BlockSpec(memory_space=pltpu.HBM)] * 2,
        out_specs=pl.BlockSpec(memory_space=pltpu.VMEM),
        scratch_shapes=[
            pltpu.VMEM((count, depth), bf16),
            pltpu.VMEM((count, width), bf16),
            pltpu.VMEM((count, width), bf16),
            pltpu.VMEM((2, half, count), bf16),
            pltpu.VMEM((half, count), bf16),
            *[pltpu.VMEM((chunks, *[2] * k, 3 * rows // 4, LANES), bf16) for k in (4, 3, 2, 1, 0)],
            *[pltpu.VMEM((chunks // 2, *[2] * k, rows // 2, LANES), bf16) for k in (4, 3, 2, 1, 0)],
            pltpu.SemaphoreType.DMA((5,)),
            pltpu.SemaphoreType.DMA((width // WIDE,)),
            pltpu.SemaphoreType.DMA((width // WIDE,)),
            pltpu.SemaphoreType.DMA((4,)),
            pltpu.SemaphoreType.DMA((4,)),
            pltpu.SemaphoreType.DMA((chunks, 4)),
            pltpu.SemaphoreType.DMA((chunks, 4)),
            pltpu.SemaphoreType.DMA((chunks // 2, 4)),
            pltpu.SemaphoreType.DMA((chunks // 2, 4)),
        ],
        compiler_params=pltpu.CompilerParams(
            collective_id=0, has_side_effects=True, vmem_limit_bytes=62 * 1024 * 1024
        ),
        cost_estimate=pl.CostEstimate(
            flops=2 * count * depth * width,
            bytes_accessed=2 * count * (depth + width) + 4 * rows * width,
            transcendentals=0,
        ),
    )(tokens, cotangent)


def shards(devices, acts, grad_out, inner_weight, first_moment, second_moment, outer_weight, outer_momentum):
    grad = gradient(acts[0], grad_out[0], devices)
    first = 0.9 * first_moment[0] + 0.1 * grad
    second = 0.95 * second_moment[0] + 0.05 * grad * grad
    first_hat = first / (1.0 - 0.9**INNER_STEP)
    second_hat = second / (1.0 - 0.95**INNER_STEP)
    inner_new = inner_weight[0] * (1.0 - 0.0004 * 0.1) - 0.0004 * first_hat / (
        jnp.sqrt(second_hat) + 1e-08
    )
    replicas = lax.axis_size("rep")
    if replicas > 1:
        inner_new = lax.psum_scatter(inner_new, "rep", scatter_dimension=0, tiled=True) / replicas
    pseudo = outer_weight - inner_new
    momentum_next = 0.9 * outer_momentum + pseudo
    outer_next = outer_weight - 0.7 * (pseudo + 0.9 * momentum_next)
    weight_next = outer_next.astype(jnp.bfloat16)
    if replicas > 1:
        weight_next = lax.all_gather(weight_next, "rep", axis=0, tiled=True)
    return (outer_next, momentum_next, weight_next)


def solution(mesh):
    placed = (
        P("rep", "fsdp", None),
        P("rep", "fsdp", None),
        P("rep", "fsdp", None),
        P("rep", "fsdp", None),
        P("rep", "fsdp", None),
        P(("fsdp", "rep"), None),
        P(("fsdp", "rep"), None),
    )
    return jax.shard_map(
        functools.partial(shards, mesh.shape["fsdp"]),
        mesh=mesh,
        in_specs=placed,
        out_specs=(P(("fsdp", "rep"), None), P(("fsdp", "rep"), None), P("fsdp", None)),
        check_vma=False,
    )
```

```python
import functools

import jax
import jax.numpy as jnp
from jax import lax
from jax.experimental import pallas as pl
from jax.experimental.pallas import tpu as pltpu
from jax.sharding import PartitionSpec as P

INNER_STEP = 500
LANES = 128
WIDE = 2 * LANES
MESH = pl.DeviceIdType.MESH

TALL = (
    (1, 4, 2, 3),
    (2, 3, 1, 4),
    (3, 2, 4, 1),
    (4, 2, 1, 3),
    (1, 2, 4, 3),
    (3, 1, 2, 4),
    (1, 2, 3, 4),
    (2, 1, 3, 4),
)
SHORT = (
    (4, 1, 2, 3),
    (2, 1, 3, 4),
    (2, 1, 3, 4),
    (1, 2, 4, 3),
)
ARRIVALS = (
    (0, 0, 0), (0, 1, 0), (1, 0, 0), (0, 2, 0), (1, 1, 0), (0, 4, 0),
    (1, 2, 0), (0, 6, 0), (0, 7, 0), (0, 3, 0), (0, 5, 0), (1, 3, 0),
    (0, 2, 1), (1, 0, 1), (1, 1, 1), (0, 4, 1), (0, 0, 1), (0, 1, 1),
    (1, 2, 1), (0, 6, 1), (1, 1, 2), (0, 2, 2), (0, 7, 1), (0, 3, 1),
    (1, 2, 2), (0, 4, 2), (0, 5, 1), (1, 3, 1), (1, 0, 2), (0, 6, 2),
    (0, 1, 2), (1, 1, 3), (0, 2, 3), (0, 0, 2), (0, 7, 2), (0, 3, 2),
    (1, 2, 3), (0, 4, 3), (0, 5, 2), (1, 0, 3), (1, 3, 2), (0, 6, 3),
    (0, 1, 3), (0, 0, 3), (0, 7, 3), (0, 3, 3), (1, 3, 3), (0, 5, 3),
)


def kernel(
    acts_hbm, cot_hbm, grad_ref,
    acts, cot, lhs,
    tall, tall0, tall1, tall2, tall3, short, short0, short1, short2, short3,
    load_sem, cot_send, cot_recv, lhs_send, lhs_recv,
    tall_send, tall_recv, short_send, short_recv,
):
    me = lax.axis_index("fsdp")
    bit = [lax.rem(me // (1 << b), 2) for b in range(5)]
    peer = [me + (1 - 2 * bit[b]) * (1 << b) for b in range(5)]
    core = bit[0]
    tokens, width = acts.shape[0], cot.shape[1]
    rows, tiles = grad_ref.shape[0], acts.shape[1] // LANES
    groups = 4
    group_rows = lhs.shape[1] // groups
    pieces = width // WIDE
    quarter = rows // 4
    kinds = (
        (TALL, tall, (tall0, tall1, tall2, tall3), tall_send, tall_recv),
        (SHORT, short, (short0, short1, short2, short3), short_send, short_recv),
    )

    span = acts.shape[1] // groups

    def acts_copy(g):
        cut = pl.ds(g * span, span)
        return pltpu.make_async_copy(acts_hbm.at[:, cut], acts.at[:, cut], load_sem.at[g])

    for g in range(groups):
        acts_copy(g).start()
    load_cot = pltpu.make_async_copy(cot_hbm, cot.at[:tokens], load_sem.at[groups])
    load_cot.start()
    barrier = pltpu.get_barrier_semaphore()
    for b in range(5):
        pl.semaphore_signal(barrier, inc=1, device_id={"fsdp": peer[b]}, device_id_type=MESH)

    def to_core(src, dst, send, recv):
        return pltpu.make_async_remote_copy(
            src_ref=src, dst_ref=dst, send_sem=send, recv_sem=recv,
            device_id={"fsdp": peer[0]}, device_id_type=MESH,
        )

    def cot_copy(j):
        cut = pl.ds(j * WIDE, WIDE)
        return to_core(cot_hbm.at[:, cut], cot.at[tokens:, cut], cot_send.at[j], cot_recv.at[j])

    def lhs_copy(g):
        cut = pl.ds(g * group_rows, group_rows)
        return to_core(
            lhs.at[1 - core, cut, :tokens], lhs.at[1 - core, cut, tokens:],
            lhs_send.at[g], lhs_recv.at[g],
        )

    for t in range(tiles):
        if t % (tiles // groups) == 0:
            acts_copy(t // (tiles // groups)).wait()
        turned = acts[:, t * LANES:(t + 1) * LANES].T
        lhs[0, t * rows:(t + 1) * rows, :tokens] = turned[:rows]
        lhs[1, t * rows:(t + 1) * rows, :tokens] = turned[rows:]
    pl.semaphore_wait(barrier, 5)
    cot_copy(0).start()
    for g in range(groups):
        lhs_copy(g).start()
    for j in range(1, pieces):
        cot_copy(j).start()

    def exchange(kind, c, s):
        orders, part, incoming, send, recv = kinds[kind]
        order = orders[c % len(orders)]
        kept = tuple(bit[b] for b in order[:s])
        return pltpu.make_async_remote_copy(
            src_ref=part.at[(c, *kept, 1 - bit[order[s]])],
            dst_ref=incoming[s].at[c],
            send_sem=send.at[c, s],
            recv_sem=recv.at[c, s],
            device_id={"fsdp": peer[order[s]]},
            device_id_type=MESH,
        )

    def place(kind, c, t):
        orders = kinds[kind][0]
        return (c, *((t >> (b - 1)) & 1 for b in orders[c % len(orders)]))

    def finish(kind, c, s):
        orders, part, incoming = kinds[kind][:3]
        order = orders[c % len(orders)]
        kept = (c, *(bit[b] for b in order[: s + 1]))
        total = part[kept].astype(jnp.float32) + incoming[s][c].astype(jnp.float32)
        if s < 3:
            part[kept] = total.astype(jnp.bfloat16)
            exchange(kind, c, s + 1).start()
        elif kind == 0:
            grad_ref[: 3 * quarter, c * LANES:(c + 1) * LANES] = total
        else:
            for h in range(2):
                strip = slice((2 * c + h) * LANES, (2 * c + h + 1) * LANES)
                grad_ref[3 * quarter:, strip] = total[h * quarter:(h + 1) * quarter]

    load_cot.wait()
    for g in range(groups):
        lhs_copy(g).wait_recv()
    for j in range(pieces):
        cot_copy(j).wait_recv()
        product = jnp.dot(
            lhs[core], cot[:, j * WIDE:(j + 1) * WIDE], preferred_element_type=jnp.float32
        ).astype(jnp.bfloat16)
        for t in range(tiles):
            for h in range(2):
                c = 2 * j + h
                cell = product[t * rows:(t + 1) * rows, h * LANES:(h + 1) * LANES]
                tall[place(0, c, t)] = cell[: 3 * quarter]
                short[(*place(1, j, t), pl.ds(h * quarter, quarter))] = cell[3 * quarter:]
        for kind, c in ((0, 2 * j), (0, 2 * j + 1), (1, j)):
            exchange(kind, c, 0).start()

    for kind, c, s in ARRIVALS:
        exchange(kind, c, s).wait_recv()
        finish(kind, c, s)
    for j in range(pieces):
        cot_copy(j).wait_send()
    for g in range(groups):
        lhs_copy(g).wait_send()
    for kind, c, s in ARRIVALS:
        exchange(kind, c, s).wait_send()


def gradient(tokens, cotangent, devices):
    count, depth = tokens.shape
    width = cotangent.shape[1]
    rows, half, chunks = depth // devices, depth // 2, width // LANES
    bf16 = jnp.bfloat16
    return pl.pallas_call(
        kernel,
        out_shape=jax.ShapeDtypeStruct((rows, width), jnp.float32),
        in_specs=[pl.BlockSpec(memory_space=pltpu.HBM)] * 2,
        out_specs=pl.BlockSpec(memory_space=pltpu.VMEM),
        scratch_shapes=[
            pltpu.VMEM((count, depth), bf16),
            pltpu.VMEM((2 * count, width), bf16),
            pltpu.VMEM((2, half, 2 * count), bf16),
            *[pltpu.VMEM((chunks, *[2] * k, 3 * rows // 4, LANES), bf16) for k in (4, 3, 2, 1, 0)],
            *[pltpu.VMEM((chunks // 2, *[2] * k, rows // 2, LANES), bf16) for k in (4, 3, 2, 1, 0)],
            pltpu.SemaphoreType.DMA((5,)),
            pltpu.SemaphoreType.DMA((width // WIDE,)),
            pltpu.SemaphoreType.DMA((width // WIDE,)),
            pltpu.SemaphoreType.DMA((4,)),
            pltpu.SemaphoreType.DMA((4,)),
            pltpu.SemaphoreType.DMA((chunks, 4)),
            pltpu.SemaphoreType.DMA((chunks, 4)),
            pltpu.SemaphoreType.DMA((chunks // 2, 4)),
            pltpu.SemaphoreType.DMA((chunks // 2, 4)),
        ],
        compiler_params=pltpu.CompilerParams(
            collective_id=0, has_side_effects=True, vmem_limit_bytes=62 * 1024 * 1024
        ),
        cost_estimate=pl.CostEstimate(
            flops=2 * count * depth * width,
            bytes_accessed=2 * count * (depth + width) + 4 * rows * width,
            transcendentals=0,
        ),
    )(tokens, cotangent)


def shards(devices, acts, grad_out, inner_weight, first_moment, second_moment, outer_weight, outer_momentum):
    grad = gradient(acts[0], grad_out[0], devices)
    first = 0.9 * first_moment[0] + 0.1 * grad
    second = 0.95 * second_moment[0] + 0.05 * grad * grad
    first_hat = first / (1.0 - 0.9**INNER_STEP)
    second_hat = second / (1.0 - 0.95**INNER_STEP)
    inner_new = inner_weight[0] * (1.0 - 0.0004 * 0.1) - 0.0004 * first_hat / (
        jnp.sqrt(second_hat) + 1e-08
    )
    replicas = lax.axis_size("rep")
    if replicas > 1:
        inner_new = lax.psum_scatter(inner_new, "rep", scatter_dimension=0, tiled=True) / replicas
    pseudo = outer_weight - inner_new
    momentum_next = 0.9 * outer_momentum + pseudo
    outer_next = outer_weight - 0.7 * (pseudo + 0.9 * momentum_next)
    weight_next = outer_next.astype(jnp.bfloat16)
    if replicas > 1:
        weight_next = lax.all_gather(weight_next, "rep", axis=0, tiled=True)
    return (outer_next, momentum_next, weight_next)


def solution(mesh):
    placed = (
        P("rep", "fsdp", None),
        P("rep", "fsdp", None),
        P("rep", "fsdp", None),
        P("rep", "fsdp", None),
        P("rep", "fsdp", None),
        P(("fsdp", "rep"), None),
        P(("fsdp", "rep"), None),
    )
    return jax.shard_map(
        functools.partial(shards, mesh.shape["fsdp"]),
        mesh=mesh,
        in_specs=placed,
        out_specs=(P(("fsdp", "rep"), None), P(("fsdp", "rep"), None), P("fsdp", None)),
        check_vma=False,
    )
```

```python
import functools

import jax
import jax.numpy as jnp
from jax import lax
from jax.experimental import pallas as pl
from jax.experimental.pallas import tpu as pltpu
from jax.sharding import PartitionSpec as P

INNER_STEP = 500
LANES = 128
WIDE = 2 * LANES
MESH = pl.DeviceIdType.MESH

TALL = (
    ((4,), (1,), (2,), (3,)),
    ((2,), (1,), (4,), (3,)),
    ((3,), (1, 2), (4,)),
    ((2,), (3,), (1,), (4,)),
    ((1,), (2,), (3, 4)),
    ((2,), (1,), (3, 4)),
    ((1,), (2,), (3, 4)),
    ((3,), (1, 2), (4,)),
)
SHORT = (
    ((3,), (4,), (1,), (2,)),
    ((1,), (2,), (3, 4)),
    ((4,), (1,), (3,), (2,)),
    ((1,), (2,), (3,), (4,)),
)
ARRIVALS = (
    (1, 1, 0), (0, 1, 0), (1, 0, 0), (0, 3, 0), (1, 3, 0), (0, 5, 0),
    (1, 1, 1), (0, 4, 0), (1, 2, 0), (0, 6, 0), (0, 0, 0), (0, 1, 1),
    (1, 3, 1), (0, 2, 0), (0, 5, 1), (1, 1, 2), (0, 7, 0), (1, 2, 1),
    (0, 4, 1), (1, 0, 1), (0, 6, 1), (0, 0, 1), (0, 3, 1), (1, 3, 2),
    (0, 1, 2), (0, 2, 1), (0, 5, 2), (0, 7, 1), (1, 0, 2), (0, 0, 2),
    (0, 3, 2), (1, 2, 2), (0, 4, 2), (1, 3, 3), (0, 6, 2), (0, 1, 3),
    (1, 0, 3), (0, 2, 2), (0, 7, 2), (0, 0, 3), (1, 2, 3), (0, 3, 3),
)


def flips(block):
    return [
        tuple(b for i, b in enumerate(block) if mask >> i & 1) for mask in range(1, 1 << len(block))
    ]


def kernel(
    acts_hbm, cot_hbm, grad_ref,
    acts, cot, lhs,
    tall, tall_in, short, short_in,
    load_sem, cot_send, cot_recv, lhs_send, lhs_recv,
    tall_send, tall_recv, short_send, short_recv,
):
    me = lax.axis_index("fsdp")
    bit = [lax.rem(me // (1 << b), 2) for b in range(5)]
    step = [(1 - 2 * bit[b]) * (1 << b) for b in range(5)]
    partners = sorted({p for rounds in TALL + SHORT for block in rounds for p in flips(block)})

    def device(flipped):
        return {"fsdp": me + sum(step[b] for b in flipped)}

    core = bit[0]
    tokens, width = acts.shape[0], cot.shape[1]
    rows, tiles = grad_ref.shape[0], acts.shape[1] // LANES
    groups = 4
    group_rows = lhs.shape[1] // groups
    pieces = width // WIDE
    quarter = rows // 4
    kinds = (
        (TALL, tall, tall_in, tall_send, tall_recv),
        (SHORT, short, short_in, short_send, short_recv),
    )

    span = acts.shape[1] // groups

    def acts_copy(g):
        cut = pl.ds(g * span, span)
        return pltpu.make_async_copy(acts_hbm.at[:, cut], acts.at[:, cut], load_sem.at[g])

    for g in range(groups):
        acts_copy(g).start()
    load_cot = pltpu.make_async_copy(cot_hbm, cot.at[:tokens], load_sem.at[groups])
    load_cot.start()
    barrier = pltpu.get_barrier_semaphore()
    for flipped in [(0,)] + partners:
        pl.semaphore_signal(barrier, inc=1, device_id=device(flipped), device_id_type=MESH)

    def to_core(src, dst, send, recv):
        return pltpu.make_async_remote_copy(
            src_ref=src, dst_ref=dst, send_sem=send, recv_sem=recv,
            device_id=device((0,)), device_id_type=MESH,
        )

    def cot_copy(j):
        cut = pl.ds(j * WIDE, WIDE)
        return to_core(cot_hbm.at[:, cut], cot.at[tokens:, cut], cot_send.at[j], cot_recv.at[j])

    def lhs_copy(g):
        cut = pl.ds(g * group_rows, group_rows)
        return to_core(
            lhs.at[1 - core, cut, :tokens], lhs.at[1 - core, cut, tokens:],
            lhs_send.at[g], lhs_recv.at[g],
        )

    for t in range(tiles):
        if t % (tiles // groups) == 0:
            acts_copy(t // (tiles // groups)).wait()
        turned = acts[:, t * LANES:(t + 1) * LANES].T
        lhs[0, t * rows:(t + 1) * rows, :tokens] = turned[:rows]
        lhs[1, t * rows:(t + 1) * rows, :tokens] = turned[rows:]
    pl.semaphore_wait(barrier, 1 + len(partners))
    cot_copy(0).start()
    for g in range(groups):
        lhs_copy(g).start()
    for j in range(1, pieces):
        cot_copy(j).start()

    def exchanges(kind, c, s):
        rounds, part, incoming, send, recv = kinds[kind]
        rounds = rounds[c % len(rounds)]
        done = [b for block in rounds[:s] for b in block]
        slot, count, copies = 16 - (16 >> len(done)), 16 >> (len(done) + len(rounds[s])), []
        sem = sum(len(flips(block)) for block in rounds[:s])
        for flipped in flips(rounds[s]):
            start = 0
            for i, b in enumerate(done + list(rounds[s])):
                start += (1 - bit[b] if b in flipped else bit[b]) * (8 >> i)
            copies.append(pltpu.make_async_remote_copy(
                src_ref=part.at[c, pl.ds(start, count)],
                dst_ref=incoming.at[c, pl.ds(slot, count)],
                send_sem=send.at[c, sem],
                recv_sem=recv.at[c, sem],
                device_id=device(flipped),
                device_id_type=MESH,
            ))
            slot, sem = slot + count, sem + 1
        return copies

    def place(kind, c, t):
        rounds = kinds[kind][0]
        bits = [b for block in rounds[c % len(rounds)] for b in block]
        return c, sum((t >> (b - 1) & 1) * (8 >> i) for i, b in enumerate(bits))

    def finish(kind, c, s):
        rounds, part, incoming = kinds[kind][:3]
        rounds = rounds[c % len(rounds)]
        done = [b for block in rounds[:s] for b in block]
        slot = 16 - (16 >> len(done))
        count = 16 >> (len(done) + len(rounds[s]))
        start = sum(bit[b] * (8 >> i) for i, b in enumerate(done + list(rounds[s])))
        kept = (c, pl.ds(start, count))
        terms = [part[kept]]
        for i in range(len(flips(rounds[s]))):
            terms.append(incoming[c, slot + i * count:slot + (i + 1) * count])
        if s + 1 == len(rounds):
            terms = [term[0].astype(jnp.float32) for term in terms]
        while len(terms) > 1:
            terms = [sum(terms[i + 1:i + 2], terms[i]) for i in range(0, len(terms), 2)]
        total = terms[0]
        if s + 1 < len(rounds):
            part[kept] = total
            for copy in exchanges(kind, c, s + 1):
                copy.start()
        elif kind == 0:
            grad_ref[: 3 * quarter, c * LANES:(c + 1) * LANES] = total
        else:
            for h in range(2):
                strip = slice((2 * c + h) * LANES, (2 * c + h + 1) * LANES)
                grad_ref[3 * quarter:, strip] = total[h * quarter:(h + 1) * quarter]

    load_cot.wait()
    for g in range(groups):
        lhs_copy(g).wait_recv()
    for j in range(pieces):
        cot_copy(j).wait_recv()
        product = jnp.dot(
            lhs[core], cot[:, j * WIDE:(j + 1) * WIDE], preferred_element_type=jnp.float32
        ).astype(jnp.bfloat16)
        for t in range(tiles):
            for h in range(2):
                c = 2 * j + h
                cell = product[t * rows:(t + 1) * rows, h * LANES:(h + 1) * LANES]
                tall[place(0, c, t)] = cell[: 3 * quarter]
                short[(*place(1, j, t), pl.ds(h * quarter, quarter))] = cell[3 * quarter:]
        for kind, c in ((0, 2 * j), (0, 2 * j + 1), (1, j)):
            for copy in exchanges(kind, c, 0):
                copy.start()

    for kind, c, s in ARRIVALS:
        for copy in exchanges(kind, c, s):
            copy.wait_recv()
        finish(kind, c, s)
    for j in range(pieces):
        cot_copy(j).wait_send()
    for g in range(groups):
        lhs_copy(g).wait_send()
    for kind, c, s in ARRIVALS:
        for copy in exchanges(kind, c, s):
            copy.wait_send()


def gradient(tokens, cotangent, devices):
    count, depth = tokens.shape
    width = cotangent.shape[1]
    rows, half, chunks = depth // devices, depth // 2, width // LANES
    bf16 = jnp.bfloat16
    return pl.pallas_call(
        kernel,
        out_shape=jax.ShapeDtypeStruct((rows, width), jnp.float32),
        in_specs=[pl.BlockSpec(memory_space=pltpu.HBM)] * 2,
        out_specs=pl.BlockSpec(memory_space=pltpu.VMEM),
        scratch_shapes=[
            pltpu.VMEM((count, depth), bf16),
            pltpu.VMEM((2 * count, width), bf16),
            pltpu.VMEM((2, half, 2 * count), bf16),
            pltpu.VMEM((chunks, 16, 3 * rows // 4, LANES), bf16),
            pltpu.VMEM((chunks, 15, 3 * rows // 4, LANES), bf16),
            pltpu.VMEM((chunks // 2, 16, rows // 2, LANES), bf16),
            pltpu.VMEM((chunks // 2, 15, rows // 2, LANES), bf16),
            pltpu.SemaphoreType.DMA((5,)),
            pltpu.SemaphoreType.DMA((width // WIDE,)),
            pltpu.SemaphoreType.DMA((width // WIDE,)),
            pltpu.SemaphoreType.DMA((4,)),
            pltpu.SemaphoreType.DMA((4,)),
            pltpu.SemaphoreType.DMA((chunks, 6)),
            pltpu.SemaphoreType.DMA((chunks, 6)),
            pltpu.SemaphoreType.DMA((chunks // 2, 6)),
            pltpu.SemaphoreType.DMA((chunks // 2, 6)),
        ],
        compiler_params=pltpu.CompilerParams(
            collective_id=0, has_side_effects=True, vmem_limit_bytes=62 * 1024 * 1024
        ),
        cost_estimate=pl.CostEstimate(
            flops=2 * count * depth * width,
            bytes_accessed=2 * count * (depth + width) + 4 * rows * width,
            transcendentals=0,
        ),
    )(tokens, cotangent)


def shards(devices, acts, grad_out, inner_weight, first_moment, second_moment, outer_weight, outer_momentum):
    grad = gradient(acts[0], grad_out[0], devices)
    first = 0.9 * first_moment[0] + 0.1 * grad
    second = 0.95 * second_moment[0] + 0.05 * grad * grad
    first_hat = first / (1.0 - 0.9**INNER_STEP)
    second_hat = second / (1.0 - 0.95**INNER_STEP)
    inner_new = inner_weight[0] * (1.0 - 0.0004 * 0.1) - 0.0004 * first_hat / (
        jnp.sqrt(second_hat) + 1e-08
    )
    replicas = lax.axis_size("rep")
    if replicas > 1:
        inner_new = lax.psum_scatter(inner_new, "rep", scatter_dimension=0, tiled=True) / replicas
    pseudo = outer_weight - inner_new
    momentum_next = 0.9 * outer_momentum + pseudo
    outer_next = outer_weight - 0.7 * (pseudo + 0.9 * momentum_next)
    weight_next = outer_next.astype(jnp.bfloat16)
    if replicas > 1:
        weight_next = lax.all_gather(weight_next, "rep", axis=0, tiled=True)
    return (outer_next, momentum_next, weight_next)


def solution(mesh):
    placed = (
        P("rep", "fsdp", None),
        P("rep", "fsdp", None),
        P("rep", "fsdp", None),
        P("rep", "fsdp", None),
        P("rep", "fsdp", None),
        P(("fsdp", "rep"), None),
        P(("fsdp", "rep"), None),
    )
    return jax.shard_map(
        functools.partial(shards, mesh.shape["fsdp"]),
        mesh=mesh,
        in_specs=placed,
        out_specs=(P(("fsdp", "rep"), None), P(("fsdp", "rep"), None), P("fsdp", None)),
        check_vma=False,
    )
```

```python
import functools

import jax
import jax.numpy as jnp
from jax import lax
from jax.experimental import pallas as pl
from jax.experimental.pallas import tpu as pltpu
from jax.sharding import PartitionSpec as P

INNER_STEP = 500
LANES = 128
WIDE = 2 * LANES
MESH = pl.DeviceIdType.MESH

TALL = (
    ((1,), (4,), (2,), (3,)),
    ((2,), (3,), (1,), (4,)),
    ((3,), (2,), (4,), (1,)),
    ((4,), (2,), (1,), (3,)),
    ((1,), (2,), (4,), (3,)),
    ((3,), (1,), (2,), (4,)),
    ((1,), (2,), (3,), (4,)),
    ((2,), (1,), (3,), (4,)),
)
SHORT = (
    ((4,), (1,), (2,), (3,)),
    ((2,), (1,), (3,), (4,)),
    ((2,), (1,), (3,), (4,)),
    ((1,), (2,), (4,), (3,)),
)
ARRIVALS = (
    (0, 0, 0), (0, 1, 0), (1, 0, 0), (0, 2, 0), (1, 1, 0), (0, 4, 0),
    (1, 2, 0), (0, 6, 0), (0, 7, 0), (0, 3, 0), (0, 5, 0), (1, 3, 0),
    (0, 2, 1), (1, 0, 1), (1, 1, 1), (0, 4, 1), (0, 0, 1), (0, 1, 1),
    (1, 2, 1), (0, 6, 1), (1, 1, 2), (0, 2, 2), (0, 7, 1), (0, 3, 1),
    (1, 2, 2), (0, 4, 2), (0, 5, 1), (1, 3, 1), (1, 0, 2), (0, 6, 2),
    (0, 1, 2), (1, 1, 3), (0, 2, 3), (0, 0, 2), (0, 7, 2), (0, 3, 2),
    (1, 2, 3), (0, 4, 3), (0, 5, 2), (1, 0, 3), (1, 3, 2), (0, 6, 3),
    (0, 1, 3), (0, 0, 3), (0, 7, 3), (0, 3, 3), (1, 3, 3), (0, 5, 3),
)


def flips(block):
    return [
        tuple(b for i, b in enumerate(block) if mask >> i & 1) for mask in range(1, 1 << len(block))
    ]


def kernel(
    acts_hbm, cot_hbm, grad_ref,
    acts, cot, lhs, ahead,
    tall, tall_in, short, short_in,
    load_sem, cot_send, cot_recv, lhs_send, lhs_recv,
    tall_send, tall_recv, short_send, short_recv,
):
    me = lax.axis_index("fsdp")
    bit = [lax.rem(me // (1 << b), 2) for b in range(5)]
    step = [(1 - 2 * bit[b]) * (1 << b) for b in range(5)]
    partners = sorted({p for rounds in TALL + SHORT for block in rounds for p in flips(block)})

    def device(flipped):
        return {"fsdp": me + sum(step[b] for b in flipped)}

    core = bit[0]
    tokens, width = acts.shape[0], cot.shape[1]
    rows, tiles = grad_ref.shape[0], acts.shape[1] // LANES
    groups = 4
    group_rows = lhs.shape[1] // groups
    pieces = width // WIDE
    quarter = rows // 4
    kinds = (
        (TALL, tall, tall_in, tall_send, tall_recv),
        (SHORT, short, short_in, short_send, short_recv),
    )

    span = acts.shape[1] // groups

    def acts_copy(g):
        cut = pl.ds(g * span, span)
        return pltpu.make_async_copy(acts_hbm.at[:, cut], acts.at[:, cut], load_sem.at[g])

    for g in range(groups):
        acts_copy(g).start()
    load_cot = pltpu.make_async_copy(cot_hbm, cot.at[:tokens], load_sem.at[groups])
    load_cot.start()
    barrier = pltpu.get_barrier_semaphore()
    for flipped in [(0,)] + partners:
        pl.semaphore_signal(barrier, inc=1, device_id=device(flipped), device_id_type=MESH)

    def to_core(src, dst, send, recv):
        return pltpu.make_async_remote_copy(
            src_ref=src, dst_ref=dst, send_sem=send, recv_sem=recv,
            device_id=device((0,)), device_id_type=MESH,
        )

    def cot_copy(j):
        cut = pl.ds(j * WIDE, WIDE)
        return to_core(cot_hbm.at[:, cut], cot.at[tokens:, cut], cot_send.at[j], cot_recv.at[j])

    def lhs_copy(g):
        cut = pl.ds(g * group_rows, group_rows)
        return to_core(
            lhs.at[1 - core, cut, :tokens], lhs.at[1 - core, cut, tokens:],
            lhs_send.at[g], lhs_recv.at[g],
        )

    def start_group(g):
        lhs_copy(g).start()
        if g == 1:
            cot_copy(0).start()

    for g in range(groups):
        acts_copy(g).wait()
        for t in range(g * tiles // groups, (g + 1) * tiles // groups):
            turned = acts[:, t * LANES:(t + 1) * LANES].T
            lhs[0, t * rows:(t + 1) * rows, :tokens] = turned[:rows]
            lhs[1, t * rows:(t + 1) * rows, :tokens] = turned[rows:]
        if g == 1:
            pl.semaphore_wait(barrier, 1 + len(partners))
            start_group(0)
        if g >= 1:
            start_group(g)
    for j in range(1, pieces):
        cot_copy(j).start()

    def exchanges(kind, c, s):
        rounds, part, incoming, send, recv = kinds[kind]
        rounds = rounds[c % len(rounds)]
        done = [b for block in rounds[:s] for b in block]
        slot, count, copies = 16 - (16 >> len(done)), 16 >> (len(done) + len(rounds[s])), []
        sem = sum(len(flips(block)) for block in rounds[:s])
        for flipped in flips(rounds[s]):
            start = 0
            for i, b in enumerate(done + list(rounds[s])):
                start += (1 - bit[b] if b in flipped else bit[b]) * (8 >> i)
            copies.append(pltpu.make_async_remote_copy(
                src_ref=part.at[c, pl.ds(start, count)],
                dst_ref=incoming.at[c, pl.ds(slot, count)],
                send_sem=send.at[c, sem],
                recv_sem=recv.at[c, sem],
                device_id=device(flipped),
                device_id_type=MESH,
            ))
            slot, sem = slot + count, sem + 1
        return copies

    def place(kind, c, t):
        rounds = kinds[kind][0]
        bits = [b for block in rounds[c % len(rounds)] for b in block]
        return c, sum((t >> (b - 1) & 1) * (8 >> i) for i, b in enumerate(bits))

    def finish(kind, c, s):
        rounds, part, incoming = kinds[kind][:3]
        rounds = rounds[c % len(rounds)]
        done = [b for block in rounds[:s] for b in block]
        slot = 16 - (16 >> len(done))
        count = 16 >> (len(done) + len(rounds[s]))
        start = sum(bit[b] * (8 >> i) for i, b in enumerate(done + list(rounds[s])))
        kept = (c, pl.ds(start, count))
        terms = [part[kept]]
        for i in range(len(flips(rounds[s]))):
            terms.append(incoming[c, slot + i * count:slot + (i + 1) * count])
        if s + 1 == len(rounds):
            terms = [term[0].astype(jnp.float32) for term in terms]
        while len(terms) > 1:
            terms = [sum(terms[i + 1:i + 2], terms[i]) for i in range(0, len(terms), 2)]
        total = terms[0]
        if s + 1 < len(rounds):
            part[kept] = total
            for copy in exchanges(kind, c, s + 1):
                copy.start()
        elif kind == 0:
            grad_ref[: 3 * quarter, c * LANES:(c + 1) * LANES] = total
        else:
            for h in range(2):
                strip = slice((2 * c + h) * LANES, (2 * c + h + 1) * LANES)
                grad_ref[3 * quarter:, strip] = total[h * quarter:(h + 1) * quarter]

    def multiply(token_range, j):
        return jnp.dot(
            lhs[core, :, token_range], cot[token_range, j * WIDE:(j + 1) * WIDE],
            preferred_element_type=jnp.float32,
        )

    load_cot.wait()
    early = ahead.shape[0]
    for j in range(early):
        ahead[j] = multiply(slice(0, tokens), j)
    for g in range(groups):
        lhs_copy(g).wait_recv()
    for j in range(pieces):
        cot_copy(j).wait_recv()
        if j < early:
            product = ahead[j] + multiply(slice(tokens, 2 * tokens), j)
        else:
            product = multiply(slice(0, 2 * tokens), j)
        product = product.astype(jnp.bfloat16)
        for t in range(tiles):
            for h in range(2):
                c = 2 * j + h
                cell = product[t * rows:(t + 1) * rows, h * LANES:(h + 1) * LANES]
                tall[place(0, c, t)] = cell[: 3 * quarter]
                short[(*place(1, j, t), pl.ds(h * quarter, quarter))] = cell[3 * quarter:]
        for kind, c in ((0, 2 * j), (0, 2 * j + 1), (1, j)):
            for copy in exchanges(kind, c, 0):
                copy.start()

    for kind, c, s in ARRIVALS:
        for copy in exchanges(kind, c, s):
            copy.wait_recv()
        finish(kind, c, s)
    for j in range(pieces):
        cot_copy(j).wait_send()
    for g in range(groups):
        lhs_copy(g).wait_send()
    for kind, c, s in ARRIVALS:
        for copy in exchanges(kind, c, s):
            copy.wait_send()


def gradient(tokens, cotangent, devices):
    count, depth = tokens.shape
    width = cotangent.shape[1]
    rows, half, chunks = depth // devices, depth // 2, width // LANES
    bf16 = jnp.bfloat16
    return pl.pallas_call(
        kernel,
        out_shape=jax.ShapeDtypeStruct((rows, width), jnp.float32),
        in_specs=[pl.BlockSpec(memory_space=pltpu.HBM)] * 2,
        out_specs=pl.BlockSpec(memory_space=pltpu.VMEM),
        scratch_shapes=[
            pltpu.VMEM((count, depth), bf16),
            pltpu.VMEM((2 * count, width), bf16),
            pltpu.VMEM((2, half, 2 * count), bf16),
            pltpu.VMEM((2, half, WIDE), jnp.float32),
            pltpu.VMEM((chunks, 16, 3 * rows // 4, LANES), bf16),
            pltpu.VMEM((chunks, 15, 3 * rows // 4, LANES), bf16),
            pltpu.VMEM((chunks // 2, 16, rows // 2, LANES), bf16),
            pltpu.VMEM((chunks // 2, 15, rows // 2, LANES), bf16),
            pltpu.SemaphoreType.DMA((5,)),
            pltpu.SemaphoreType.DMA((width // WIDE,)),
            pltpu.SemaphoreType.DMA((width // WIDE,)),
            pltpu.SemaphoreType.DMA((4,)),
            pltpu.SemaphoreType.DMA((4,)),
            pltpu.SemaphoreType.DMA((chunks, 6)),
            pltpu.SemaphoreType.DMA((chunks, 6)),
            pltpu.SemaphoreType.DMA((chunks // 2, 6)),
            pltpu.SemaphoreType.DMA((chunks // 2, 6)),
        ],
        compiler_params=pltpu.CompilerParams(
            collective_id=0, has_side_effects=True, vmem_limit_bytes=62 * 1024 * 1024
        ),
        cost_estimate=pl.CostEstimate(
            flops=2 * count * depth * width,
            bytes_accessed=2 * count * (depth + width) + 4 * rows * width,
            transcendentals=0,
        ),
    )(tokens, cotangent)


def shards(devices, acts, grad_out, inner_weight, first_moment, second_moment, outer_weight, outer_momentum):
    grad = gradient(acts[0], grad_out[0], devices)
    first = 0.9 * first_moment[0] + 0.1 * grad
    second = 0.95 * second_moment[0] + 0.05 * grad * grad
    first_hat = first / (1.0 - 0.9**INNER_STEP)
    second_hat = second / (1.0 - 0.95**INNER_STEP)
    inner_new = inner_weight[0] * (1.0 - 0.0004 * 0.1) - 0.0004 * first_hat / (
        jnp.sqrt(second_hat) + 1e-08
    )
    replicas = lax.axis_size("rep")
    if replicas > 1:
        inner_new = lax.psum_scatter(inner_new, "rep", scatter_dimension=0, tiled=True) / replicas
    pseudo = outer_weight - inner_new
    momentum_next = 0.9 * outer_momentum + pseudo
    outer_next = outer_weight - 0.7 * (pseudo + 0.9 * momentum_next)
    weight_next = outer_next.astype(jnp.bfloat16)
    if replicas > 1:
        weight_next = lax.all_gather(weight_next, "rep", axis=0, tiled=True)
    return (outer_next, momentum_next, weight_next)


def solution(mesh):
    placed = (
        P("rep", "fsdp", None),
        P("rep", "fsdp", None),
        P("rep", "fsdp", None),
        P("rep", "fsdp", None),
        P("rep", "fsdp", None),
        P(("fsdp", "rep"), None),
        P(("fsdp", "rep"), None),
    )
    return jax.shard_map(
        functools.partial(shards, mesh.shape["fsdp"]),
        mesh=mesh,
        in_specs=placed,
        out_specs=(P(("fsdp", "rep"), None), P(("fsdp", "rep"), None), P("fsdp", None)),
        check_vma=False,
    )
```

```python
import functools

import jax
import jax.numpy as jnp
from jax import lax
from jax.experimental import pallas as pl
from jax.experimental.pallas import tpu as pltpu
from jax.sharding import PartitionSpec as P

INNER_STEP = 500
LANES = 128
WIDE = 2 * LANES
MESH = pl.DeviceIdType.MESH

ORDERS = ((1, 2, 3, 4), (2, 1, 3, 4), (3, 1, 2, 4))


def kernel(
    acts_hbm, cot_hbm, grad_ref,
    acts, cot, lhs, left, right, low, left_in, right_in, low_in,
    load_sem, cot_send, cot_recv, lhs_send, lhs_recv, send_sem, recv_sem,
):
    me = lax.axis_index("fsdp")
    bit = [lax.rem(me // (1 << b), 2) for b in range(5)]
    peer = [{"fsdp": me + (1 - 2 * bit[b]) * (1 << b)} for b in range(5)]
    core = bit[0]
    tokens, width = acts.shape[0], cot.shape[1]
    rows, tiles = grad_ref.shape[0], acts.shape[1] // LANES
    groups = 4
    group_rows, group_tiles = lhs.shape[1] // groups, tiles // groups
    pieces = width // WIDE
    quarter = rows // 4
    parts, incoming = (left, right, low), (left_in, right_in, low_in)
    span = acts.shape[1] // groups

    def each(count, body):
        def run(i, carry):
            body(i)
            return carry

        lax.fori_loop(0, count, run, 0)

    def lanes(i, size):
        return pl.ds(pl.multiple_of(i * size, size), size)

    def acts_copy(g):
        cut = lanes(g, span)
        return pltpu.make_async_copy(acts_hbm.at[:, cut], acts.at[:, cut], load_sem.at[g])

    each(groups, lambda g: acts_copy(g).start())
    load_cot = pltpu.make_async_copy(cot_hbm, cot.at[:tokens], load_sem.at[groups])
    load_cot.start()
    barrier = pltpu.get_barrier_semaphore()
    for b in range(5):
        pl.semaphore_signal(barrier, inc=1, device_id=peer[b], device_id_type=MESH)

    def to_core(src, dst, send, recv):
        return pltpu.make_async_remote_copy(
            src_ref=src, dst_ref=dst, send_sem=send, recv_sem=recv,
            device_id=peer[0], device_id_type=MESH,
        )

    def cot_copy(j):
        cut = lanes(j, WIDE)
        return to_core(cot_hbm.at[:, cut], cot.at[tokens:, cut], cot_send.at[j], cot_recv.at[j])

    def lhs_copy(g):
        cut = lanes(g, group_rows)
        return to_core(
            lhs.at[1 - core, cut, :tokens], lhs.at[1 - core, cut, tokens:],
            lhs_send.at[g], lhs_recv.at[g],
        )

    def turn_group(g):
        acts_copy(g).wait()

        def turn(k):
            t = g * group_tiles + k
            turned = acts[:, lanes(t, LANES)].T
            lhs[0, lanes(t, rows), :tokens] = turned[:rows]
            lhs[1, lanes(t, rows), :tokens] = turned[rows:]

        each(group_tiles, turn)

    def turn_and_send(g):
        turn_group(g)
        lhs_copy(g).start()

    turn_group(0)
    pl.semaphore_wait(barrier, 5)
    lhs_copy(0).start()
    cot_copy(0).start()
    each(groups - 1, lambda g: turn_and_send(g + 1))
    each(pieces - 1, lambda j: cot_copy(j + 1).start())

    def exchange(kind, j, s):
        order, start = ORDERS[kind], 0
        for i in range(s):
            start += bit[order[i]] * (8 >> i)
        start += (1 - bit[order[s]]) * (8 >> s)
        return pltpu.make_async_remote_copy(
            src_ref=parts[kind].at[j, pl.ds(start, 8 >> s)],
            dst_ref=incoming[kind].at[j, pl.ds(16 - (16 >> s), 8 >> s)],
            send_sem=send_sem.at[kind, j, s],
            recv_sem=recv_sem.at[kind, j, s],
            device_id=peer[order[s]],
            device_id_type=MESH,
        )

    def place(kind, t):
        return sum((t >> (b - 1) & 1) * (8 >> i) for i, b in enumerate(ORDERS[kind]))

    def multiply(j):
        cot_copy(j).wait_recv()
        product = jnp.dot(
            lhs[core], cot[:, lanes(j, WIDE)], preferred_element_type=jnp.float32
        ).astype(jnp.bfloat16)
        for t in range(tiles):
            cell = product[t * rows:(t + 1) * rows]
            left[j, place(0, t)] = cell[: 3 * quarter, :LANES]
            right[j, place(1, t)] = cell[: 3 * quarter, LANES:]
            low[j, place(2, t), :quarter] = cell[3 * quarter:, :LANES]
            low[j, place(2, t), quarter:] = cell[3 * quarter:, LANES:]
        for kind in range(3):
            exchange(kind, j, 0).start()

    load_cot.wait()
    each(groups, lambda g: lhs_copy(g).wait_recv())
    each(pieces, multiply)

    def finish(kind, j, s):
        exchange(kind, j, s).wait_recv()
        start, count = sum(bit[b] * (8 >> i) for i, b in enumerate(ORDERS[kind][: s + 1])), 8 >> s
        ours = parts[kind][j, pl.ds(start, count)]
        theirs = incoming[kind][j, 16 - 2 * count:16 - count]
        if s < 3:
            parts[kind][j, pl.ds(start, count)] = ours + theirs
            exchange(kind, j, s + 1).start()
            return
        total = ours[0].astype(jnp.float32) + theirs[0].astype(jnp.float32)
        if kind < 2:
            grad_ref[: 3 * quarter, lanes(2 * j + kind, LANES)] = total
        else:
            grad_ref[3 * quarter:, lanes(2 * j, LANES)] = total[:quarter]
            grad_ref[3 * quarter:, lanes(2 * j + 1, LANES)] = total[quarter:]

    def finish_piece(s, j):
        for kind in range(3):
            finish(kind, j, s)

    def drain(s, j):
        for kind in range(3):
            exchange(kind, j, s).wait_send()

    for s in range(4):
        each(pieces, functools.partial(finish_piece, s))
    each(pieces, lambda j: cot_copy(j).wait_send())
    each(groups, lambda g: lhs_copy(g).wait_send())
    for s in range(4):
        each(pieces, functools.partial(drain, s))


def gradient(tokens, cotangent, devices):
    count, depth = tokens.shape
    width = cotangent.shape[1]
    rows, half, pieces = depth // devices, depth // 2, width // WIDE
    bf16 = jnp.bfloat16
    return pl.pallas_call(
        kernel,
        out_shape=jax.ShapeDtypeStruct((rows, width), jnp.float32),
        in_specs=[pl.BlockSpec(memory_space=pltpu.HBM)] * 2,
        out_specs=pl.BlockSpec(memory_space=pltpu.VMEM),
        scratch_shapes=[
            pltpu.VMEM((count, depth), bf16),
            pltpu.VMEM((2 * count, width), bf16),
            pltpu.VMEM((2, half, 2 * count), bf16),
            pltpu.VMEM((pieces, 16, 3 * rows // 4, LANES), bf16),
            pltpu.VMEM((pieces, 16, 3 * rows // 4, LANES), bf16),
            pltpu.VMEM((pieces, 16, rows // 2, LANES), bf16),
            pltpu.VMEM((pieces, 15, 3 * rows // 4, LANES), bf16),
            pltpu.VMEM((pieces, 15, 3 * rows // 4, LANES), bf16),
            pltpu.VMEM((pieces, 15, rows // 2, LANES), bf16),
            pltpu.SemaphoreType.DMA((5,)),
            pltpu.SemaphoreType.DMA((pieces,)),
            pltpu.SemaphoreType.DMA((pieces,)),
            pltpu.SemaphoreType.DMA((4,)),
            pltpu.SemaphoreType.DMA((4,)),
            pltpu.SemaphoreType.DMA((3, pieces, 4)),
            pltpu.SemaphoreType.DMA((3, pieces, 4)),
        ],
        compiler_params=pltpu.CompilerParams(
            collective_id=0, has_side_effects=True, vmem_limit_bytes=62 * 1024 * 1024
        ),
        cost_estimate=pl.CostEstimate(
            flops=2 * count * depth * width,
            bytes_accessed=2 * count * (depth + width) + 4 * rows * width,
            transcendentals=0,
        ),
    )(tokens, cotangent)


def shards(devices, acts, grad_out, inner_weight, first_moment, second_moment, outer_weight, outer_momentum):
    grad = gradient(acts[0], grad_out[0], devices)
    first = 0.9 * first_moment[0] + 0.1 * grad
    second = 0.95 * second_moment[0] + 0.05 * grad * grad
    first_hat = first / (1.0 - 0.9**INNER_STEP)
    second_hat = second / (1.0 - 0.95**INNER_STEP)
    inner_new = inner_weight[0] * (1.0 - 0.0004 * 0.1) - 0.0004 * first_hat / (
        jnp.sqrt(second_hat) + 1e-08
    )
    replicas = lax.axis_size("rep")
    if replicas > 1:
        inner_new = lax.psum_scatter(inner_new, "rep", scatter_dimension=0, tiled=True) / replicas
    pseudo = outer_weight - inner_new
    momentum_next = 0.9 * outer_momentum + pseudo
    outer_next = outer_weight - 0.7 * (pseudo + 0.9 * momentum_next)
    weight_next = outer_next.astype(jnp.bfloat16)
    if replicas > 1:
        weight_next = lax.all_gather(weight_next, "rep", axis=0, tiled=True)
    return (outer_next, momentum_next, weight_next)


def solution(mesh):
    placed = (
        P("rep", "fsdp", None),
        P("rep", "fsdp", None),
        P("rep", "fsdp", None),
        P("rep", "fsdp", None),
        P("rep", "fsdp", None),
        P(("fsdp", "rep"), None),
        P(("fsdp", "rep"), None),
    )
    return jax.shard_map(
        functools.partial(shards, mesh.shape["fsdp"]),
        mesh=mesh,
        in_specs=placed,
        out_specs=(P(("fsdp", "rep"), None), P(("fsdp", "rep"), None), P("fsdp", None)),
        check_vma=False,
    )
```

```python
import functools

import jax
import jax.numpy as jnp
from jax import lax
from jax.experimental import pallas as pl
from jax.experimental.pallas import tpu as pltpu
from jax.sharding import PartitionSpec as P

INNER_STEP = 500
LANES = 128
WIDE = 2 * LANES
MESH = pl.DeviceIdType.MESH

TALL = (
    ((1,), (4,), (2,), (3,)),
    ((2,), (3,), (1,), (4,)),
    ((3,), (2,), (4,), (1,)),
    ((4,), (2,), (1,), (3,)),
    ((1,), (2,), (4,), (3,)),
    ((3,), (1,), (2,), (4,)),
    ((1,), (2,), (3,), (4,)),
    ((2,), (1,), (3,), (4,)),
)
SHORT = (
    ((4,), (1,), (2,), (3,)),
    ((2,), (1,), (3,), (4,)),
    ((2,), (1,), (3,), (4,)),
    ((1,), (2,), (4,), (3,)),
)
ARRIVALS = (
    (0, 0, 0), (0, 1, 0), (1, 0, 0), (0, 2, 0), (1, 1, 0), (0, 4, 0),
    (1, 2, 0), (0, 6, 0), (0, 7, 0), (0, 3, 0), (0, 5, 0), (1, 3, 0),
    (0, 2, 1), (1, 0, 1), (1, 1, 1), (0, 4, 1), (0, 0, 1), (0, 1, 1),
    (1, 2, 1), (0, 6, 1), (1, 1, 2), (0, 2, 2), (0, 7, 1), (0, 3, 1),
    (1, 2, 2), (0, 4, 2), (0, 5, 1), (1, 3, 1), (1, 0, 2), (0, 6, 2),
    (0, 1, 2), (1, 1, 3), (0, 2, 3), (0, 0, 2), (0, 7, 2), (0, 3, 2),
    (1, 2, 3), (0, 4, 3), (0, 5, 2), (1, 0, 3), (1, 3, 2), (0, 6, 3),
    (0, 1, 3), (0, 0, 3), (0, 7, 3), (0, 3, 3), (1, 3, 3), (0, 5, 3),
)


def flips(block):
    return [
        tuple(b for i, b in enumerate(block) if mask >> i & 1) for mask in range(1, 1 << len(block))
    ]


def kernel(
    acts_hbm, cot_hbm, grad_ref,
    acts, cot, lhs,
    tall, tall_in, short, short_in,
    load_sem, cot_send, cot_recv, lhs_send, lhs_recv,
    tall_send, tall_recv, short_send, short_recv,
):
    me = lax.axis_index("fsdp")
    bit = [lax.rem(me // (1 << b), 2) for b in range(5)]
    step = [(1 - 2 * bit[b]) * (1 << b) for b in range(5)]
    partners = sorted({p for rounds in TALL + SHORT for block in rounds for p in flips(block)})

    def device(flipped):
        return {"fsdp": me + sum(step[b] for b in flipped)}

    core = bit[0]
    tokens, width = acts.shape[0], cot.shape[1]
    rows, tiles = grad_ref.shape[0], acts.shape[1] // LANES
    groups = 4
    group_rows = lhs.shape[1] // groups
    pieces = width // WIDE
    quarter = rows // 4
    kinds = (
        (TALL, tall, tall_in, tall_send, tall_recv),
        (SHORT, short, short_in, short_send, short_recv),
    )

    span = acts.shape[1] // groups

    def acts_copy(g):
        cut = pl.ds(g * span, span)
        return pltpu.make_async_copy(acts_hbm.at[:, cut], acts.at[:, cut], load_sem.at[g])

    for g in range(groups):
        acts_copy(g).start()
    load_cot = pltpu.make_async_copy(cot_hbm, cot.at[:tokens], load_sem.at[groups])
    load_cot.start()
    barrier = pltpu.get_barrier_semaphore()
    for flipped in [(0,)] + partners:
        pl.semaphore_signal(barrier, inc=1, device_id=device(flipped), device_id_type=MESH)

    def to_core(src, dst, send, recv):
        return pltpu.make_async_remote_copy(
            src_ref=src, dst_ref=dst, send_sem=send, recv_sem=recv,
            device_id=device((0,)), device_id_type=MESH,
        )

    def cot_copy(j):
        cut = pl.ds(j * WIDE, WIDE)
        return to_core(cot_hbm.at[:, cut], cot.at[tokens:, cut], cot_send, cot_recv.at[j])

    def lhs_copy(g):
        cut = pl.ds(g * group_rows, group_rows)
        return to_core(
            lhs.at[1 - core, cut, :tokens], lhs.at[1 - core, cut, tokens:],
            lhs_send, lhs_recv,
        )

    def start_group(g):
        lhs_copy(g).start()
        if g == 1:
            cot_copy(0).start()

    for g in range(groups):
        acts_copy(g).wait()
        for t in range(g * tiles // groups, (g + 1) * tiles // groups):
            turned = acts[:, t * LANES:(t + 1) * LANES].T
            lhs[0, t * rows:(t + 1) * rows, :tokens] = turned[:rows]
            lhs[1, t * rows:(t + 1) * rows, :tokens] = turned[rows:]
        if g == 1:
            pl.semaphore_wait(barrier, 1 + len(partners))
            start_group(0)
        if g >= 1:
            start_group(g)
    for j in range(1, pieces):
        cot_copy(j).start()

    def exchanges(kind, c, s):
        rounds, part, incoming, send, recv = kinds[kind]
        rounds = rounds[c % len(rounds)]
        done = [b for block in rounds[:s] for b in block]
        slot, count, copies = 16 - (16 >> len(done)), 16 >> (len(done) + len(rounds[s])), []
        sem = sum(len(flips(block)) for block in rounds[:s])
        for flipped in flips(rounds[s]):
            start = 0
            for i, b in enumerate(done + list(rounds[s])):
                start += (1 - bit[b] if b in flipped else bit[b]) * (8 >> i)
            copies.append(pltpu.make_async_remote_copy(
                src_ref=part.at[c, pl.ds(start, count)],
                dst_ref=incoming.at[c, pl.ds(slot, count)],
                send_sem=send,
                recv_sem=recv.at[c, sem],
                device_id=device(flipped),
                device_id_type=MESH,
            ))
            slot, sem = slot + count, sem + 1
        return copies

    def place(kind, c, t):
        rounds = kinds[kind][0]
        bits = [b for block in rounds[c % len(rounds)] for b in block]
        return c, sum((t >> (b - 1) & 1) * (8 >> i) for i, b in enumerate(bits))

    def finish(kind, c, s):
        rounds, part, incoming = kinds[kind][:3]
        rounds = rounds[c % len(rounds)]
        done = [b for block in rounds[:s] for b in block]
        slot = 16 - (16 >> len(done))
        count = 16 >> (len(done) + len(rounds[s]))
        start = sum(bit[b] * (8 >> i) for i, b in enumerate(done + list(rounds[s])))
        kept = (c, pl.ds(start, count))
        terms = [part[kept]]
        for i in range(len(flips(rounds[s]))):
            terms.append(incoming[c, slot + i * count:slot + (i + 1) * count])
        if s + 1 == len(rounds):
            terms = [term[0].astype(jnp.float32) for term in terms]
        while len(terms) > 1:
            terms = [sum(terms[i + 1:i + 2], terms[i]) for i in range(0, len(terms), 2)]
        total = terms[0]
        if s + 1 < len(rounds):
            part[kept] = total
            for copy in exchanges(kind, c, s + 1):
                copy.start()
        elif kind == 0:
            grad_ref[: 3 * quarter, c * LANES:(c + 1) * LANES] = total
        else:
            for h in range(2):
                strip = slice((2 * c + h) * LANES, (2 * c + h + 1) * LANES)
                grad_ref[3 * quarter:, strip] = total[h * quarter:(h + 1) * quarter]

    load_cot.wait()
    all_rows = lhs.at[1 - core, :, :tokens]
    to_core(all_rows, lhs.at[1 - core, :, tokens:], lhs_send, lhs_recv).wait_recv()
    for j in range(pieces):
        cot_copy(j).wait_recv()
        product = jnp.dot(
            lhs[core], cot[:, j * WIDE:(j + 1) * WIDE], preferred_element_type=jnp.float32
        )
        product = product.astype(jnp.bfloat16)
        for t in range(tiles):
            for h in range(2):
                c = 2 * j + h
                cell = product[t * rows:(t + 1) * rows, h * LANES:(h + 1) * LANES]
                tall[place(0, c, t)] = cell[: 3 * quarter]
                short[(*place(1, j, t), pl.ds(h * quarter, quarter))] = cell[3 * quarter:]
        for kind, c in ((0, 2 * j), (0, 2 * j + 1), (1, j)):
            for copy in exchanges(kind, c, 0):
                copy.start()

    for kind, c, s in ARRIVALS:
        for copy in exchanges(kind, c, s):
            copy.wait_recv()
        finish(kind, c, s)
    to_core(cot_hbm, cot.at[tokens:], cot_send, cot_recv.at[0]).wait_send()
    to_core(all_rows, lhs.at[1 - core, :, tokens:], lhs_send, lhs_recv).wait_send()
    to_core(tall_in, tall_in, tall_send, tall_recv.at[0, 0]).wait_send()
    to_core(short_in, short_in, short_send, short_recv.at[0, 0]).wait_send()


def gradient(tokens, cotangent, devices):
    count, depth = tokens.shape
    width = cotangent.shape[1]
    rows, half, chunks = depth // devices, depth // 2, width // LANES
    bf16 = jnp.bfloat16
    return pl.pallas_call(
        kernel,
        out_shape=jax.ShapeDtypeStruct((rows, width), jnp.float32),
        in_specs=[pl.BlockSpec(memory_space=pltpu.HBM)] * 2,
        out_specs=pl.BlockSpec(memory_space=pltpu.VMEM),
        scratch_shapes=[
            pltpu.VMEM((count, depth), bf16),
            pltpu.VMEM((2 * count, width), bf16),
            pltpu.VMEM((2, half, 2 * count), bf16),
            pltpu.VMEM((chunks, 16, 3 * rows // 4, LANES), bf16),
            pltpu.VMEM((chunks, 15, 3 * rows // 4, LANES), bf16),
            pltpu.VMEM((chunks // 2, 16, rows // 2, LANES), bf16),
            pltpu.VMEM((chunks // 2, 15, rows // 2, LANES), bf16),
            pltpu.SemaphoreType.DMA((5,)),
            pltpu.SemaphoreType.DMA,
            pltpu.SemaphoreType.DMA((width // WIDE,)),
            pltpu.SemaphoreType.DMA,
            pltpu.SemaphoreType.DMA,
            pltpu.SemaphoreType.DMA,
            pltpu.SemaphoreType.DMA((chunks, 4)),
            pltpu.SemaphoreType.DMA,
            pltpu.SemaphoreType.DMA((chunks // 2, 4)),
        ],
        compiler_params=pltpu.CompilerParams(
            collective_id=0, has_side_effects=True, vmem_limit_bytes=62 * 1024 * 1024
        ),
        cost_estimate=pl.CostEstimate(
            flops=2 * count * depth * width,
            bytes_accessed=2 * count * (depth + width) + 4 * rows * width,
            transcendentals=0,
        ),
    )(tokens, cotangent)


def shards(devices, acts, grad_out, inner_weight, first_moment, second_moment, outer_weight, outer_momentum):
    grad = gradient(acts[0], grad_out[0], devices)
    first = 0.9 * first_moment[0] + 0.1 * grad
    second = 0.95 * second_moment[0] + 0.05 * grad * grad
    first_hat = first / (1.0 - 0.9**INNER_STEP)
    second_hat = second / (1.0 - 0.95**INNER_STEP)
    inner_new = inner_weight[0] * (1.0 - 0.0004 * 0.1) - 0.0004 * first_hat / (
        jnp.sqrt(second_hat) + 1e-08
    )
    replicas = lax.axis_size("rep")
    if replicas > 1:
        inner_new = lax.psum_scatter(inner_new, "rep", scatter_dimension=0, tiled=True) / replicas
    pseudo = outer_weight - inner_new
    momentum_next = 0.9 * outer_momentum + pseudo
    outer_next = outer_weight - 0.7 * (pseudo + 0.9 * momentum_next)
    weight_next = outer_next.astype(jnp.bfloat16)
    if replicas > 1:
        weight_next = lax.all_gather(weight_next, "rep", axis=0, tiled=True)
    return (outer_next, momentum_next, weight_next)


def solution(mesh):
    placed = (
        P("rep", "fsdp", None),
        P("rep", "fsdp", None),
        P("rep", "fsdp", None),
        P("rep", "fsdp", None),
        P("rep", "fsdp", None),
        P(("fsdp", "rep"), None),
        P(("fsdp", "rep"), None),
    )
    return jax.shard_map(
        functools.partial(shards, mesh.shape["fsdp"]),
        mesh=mesh,
        in_specs=placed,
        out_specs=(P(("fsdp", "rep"), None), P(("fsdp", "rep"), None), P("fsdp", None)),
        check_vma=False,
    )
```

```python
import functools

import jax
import jax.numpy as jnp
from jax import lax
from jax.experimental import pallas as pl
from jax.experimental.pallas import tpu as pltpu
from jax.sharding import PartitionSpec as P

INNER_STEP = 500
LANES = 128
WIDE = 2 * LANES
MESH = pl.DeviceIdType.MESH

TALL = (
    ((1,), (4,), (2,), (3,)),
    ((2,), (3,), (1,), (4,)),
    ((3,), (2,), (4,), (1,)),
    ((4,), (2,), (1,), (3,)),
    ((1,), (2,), (4,), (3,)),
    ((3,), (1,), (2,), (4,)),
    ((1,), (2,), (3,), (4,)),
    ((2,), (1,), (3,), (4,)),
)
SHORT = (
    ((4,), (1,), (2,), (3,)),
    ((2,), (1,), (3,), (4,)),
    ((2,), (1,), (3,), (4,)),
    ((1,), (2,), (4,), (3,)),
)
ARRIVALS = (
    (0, 0, 0), (0, 1, 0), (1, 0, 0), (0, 2, 0), (1, 1, 0), (0, 4, 0),
    (1, 2, 0), (0, 6, 0), (0, 7, 0), (0, 3, 0), (0, 5, 0), (1, 3, 0),
    (0, 2, 1), (1, 0, 1), (1, 1, 1), (0, 4, 1), (0, 0, 1), (0, 1, 1),
    (1, 2, 1), (0, 6, 1), (1, 1, 2), (0, 2, 2), (0, 7, 1), (0, 3, 1),
    (1, 2, 2), (0, 4, 2), (0, 5, 1), (1, 3, 1), (1, 0, 2), (0, 6, 2),
    (0, 1, 2), (1, 1, 3), (0, 2, 3), (0, 0, 2), (0, 7, 2), (0, 3, 2),
    (1, 2, 3), (0, 4, 3), (0, 5, 2), (1, 0, 3), (1, 3, 2), (0, 6, 3),
    (0, 1, 3), (0, 0, 3), (0, 7, 3), (0, 3, 3), (1, 3, 3), (0, 5, 3),
)


def flips(block):
    return [
        tuple(b for i, b in enumerate(block) if mask >> i & 1) for mask in range(1, 1 << len(block))
    ]


def kernel(
    acts_hbm, cot_hbm, grad_ref,
    acts, cot, lhs,
    tall, tall_in, short, short_in,
    load_sem, cot_send, cot_recv, lhs_send, lhs_recv,
    tall_send, tall_recv, short_send, short_recv,
):
    me = lax.axis_index("fsdp")
    bit = [lax.rem(me // (1 << b), 2) for b in range(5)]
    step = [(1 - 2 * bit[b]) * (1 << b) for b in range(5)]
    partners = sorted({p for rounds in TALL + SHORT for block in rounds for p in flips(block)})

    def device(flipped):
        return {"fsdp": me + sum(step[b] for b in flipped)}

    core = bit[0]
    tokens, width = acts.shape[0], cot.shape[1]
    rows, tiles = grad_ref.shape[0], acts.shape[1] // LANES
    groups = 4
    group_rows = lhs.shape[1] // groups
    pieces = width // WIDE
    quarter = rows // 4
    kinds = (
        (TALL, tall, tall_in, tall_send, tall_recv),
        (SHORT, short, short_in, short_send, short_recv),
    )

    span = acts.shape[1] // groups

    def acts_copy(g):
        cut = pl.ds(g * span, span)
        return pltpu.make_async_copy(acts_hbm.at[:, cut], acts.at[:, cut], load_sem.at[g])

    for g in range(groups):
        acts_copy(g).start()
    load_cot = pltpu.make_async_copy(cot_hbm, cot.at[:tokens], load_sem.at[groups])
    load_cot.start()
    barrier = pltpu.get_barrier_semaphore()
    for flipped in [(0,)] + partners:
        pl.semaphore_signal(barrier, inc=1, device_id=device(flipped), device_id_type=MESH)

    def to_core(src, dst, send, recv):
        return pltpu.make_async_remote_copy(
            src_ref=src, dst_ref=dst, send_sem=send, recv_sem=recv,
            device_id=device((0,)), device_id_type=MESH,
        )

    def cot_copy(j):
        cut = pl.ds(j * WIDE, WIDE)
        return to_core(cot_hbm.at[:, cut], cot.at[tokens:, cut], cot_send, cot_recv.at[j])

    def lhs_copy(g):
        cut = pl.ds(g * group_rows, group_rows)
        return to_core(
            lhs.at[1 - core, cut, :tokens], lhs.at[1 - core, cut, tokens:],
            lhs_send, lhs_recv,
        )

    def start_group(g):
        lhs_copy(g).start()
        if g == 1:
            cot_copy(0).start()

    for g in range(groups):
        acts_copy(g).wait()
        for t in range(g * tiles // groups, (g + 1) * tiles // groups):
            turned = acts[:, t * LANES:(t + 1) * LANES].T
            lhs[0, t * rows:(t + 1) * rows, :tokens] = turned[:rows]
            lhs[1, t * rows:(t + 1) * rows, :tokens] = turned[rows:]
        if g == 1:
            pl.semaphore_wait(barrier, 1 + len(partners))
            start_group(0)
        if g >= 1:
            start_group(g)
    for j in range(1, pieces):
        cot_copy(j).start()

    def exchanges(kind, c, s):
        rounds, part, incoming, send, recv = kinds[kind]
        rounds = rounds[c % len(rounds)]
        done = [b for block in rounds[:s] for b in block]
        slot, count, copies = 16 - (16 >> len(done)), 16 >> (len(done) + len(rounds[s])), []
        sem = sum(len(flips(block)) for block in rounds[:s])
        for flipped in flips(rounds[s]):
            start = 0
            for i, b in enumerate(done + list(rounds[s])):
                start += (1 - bit[b] if b in flipped else bit[b]) * (8 >> i)
            copies.append(pltpu.make_async_remote_copy(
                src_ref=part.at[c, pl.ds(start, count)],
                dst_ref=incoming.at[c, pl.ds(slot, count)],
                send_sem=send,
                recv_sem=recv.at[c, sem],
                device_id=device(flipped),
                device_id_type=MESH,
            ))
            slot, sem = slot + count, sem + 1
        return copies

    def place(kind, c, t):
        rounds = kinds[kind][0]
        bits = [b for block in rounds[c % len(rounds)] for b in block]
        return c, sum((t >> (b - 1) & 1) * (8 >> i) for i, b in enumerate(bits))

    def finish(kind, c, s):
        rounds, part, incoming = kinds[kind][:3]
        rounds = rounds[c % len(rounds)]
        done = [b for block in rounds[:s] for b in block]
        slot = 16 - (16 >> len(done))
        count = 16 >> (len(done) + len(rounds[s]))
        start = sum(bit[b] * (8 >> i) for i, b in enumerate(done + list(rounds[s])))
        kept = (c, pl.ds(start, count))
        terms = [part[kept]]
        for i in range(len(flips(rounds[s]))):
            terms.append(incoming[c, slot + i * count:slot + (i + 1) * count])
        if s + 1 == len(rounds):
            terms = [term[0].astype(jnp.float32) for term in terms]
        while len(terms) > 1:
            terms = [sum(terms[i + 1:i + 2], terms[i]) for i in range(0, len(terms), 2)]
        total = terms[0]
        if s + 1 < len(rounds):
            part[kept] = total
            for copy in exchanges(kind, c, s + 1):
                copy.start()
        elif kind == 0:
            grad_ref[: 3 * quarter, c * LANES:(c + 1) * LANES] = total
        else:
            for h in range(2):
                strip = slice((2 * c + h) * LANES, (2 * c + h + 1) * LANES)
                grad_ref[3 * quarter:, strip] = total[h * quarter:(h + 1) * quarter]

    load_cot.wait()
    all_rows = lhs.at[1 - core, :, :tokens]
    to_core(all_rows, lhs.at[1 - core, :, tokens:], lhs_send, lhs_recv).wait_recv()
    for j in range(pieces):
        cot_copy(j).wait_recv()
        product = jnp.dot(
            lhs[core], cot[:, j * WIDE:(j + 1) * WIDE], preferred_element_type=jnp.float32
        )
        product = product.astype(jnp.bfloat16)
        for t in range(tiles):
            for h in range(2):
                c = 2 * j + h
                cell = product[t * rows:(t + 1) * rows, h * LANES:(h + 1) * LANES]
                tall[place(0, c, t)] = cell[: 3 * quarter]
                short[(*place(1, j, t), pl.ds(h * quarter, quarter))] = cell[3 * quarter:]
        for kind, c in ((0, 2 * j), (0, 2 * j + 1), (1, j)):
            for copy in exchanges(kind, c, 0):
                copy.start()

    for kind, c, s in ARRIVALS:
        for copy in exchanges(kind, c, s):
            copy.wait_recv()
        finish(kind, c, s)
    to_core(cot_hbm, cot.at[tokens:], cot_send, cot_recv.at[0]).wait_send()
    to_core(all_rows, lhs.at[1 - core, :, tokens:], lhs_send, lhs_recv).wait_send()
    to_core(tall_in, tall_in, tall_send, tall_recv.at[0, 0]).wait_send()
    to_core(short_in, short_in, short_send, short_recv.at[0, 0]).wait_send()


def gradient(tokens, cotangent, devices):
    count, depth = tokens.shape
    width = cotangent.shape[1]
    rows, half, chunks = depth // devices, depth // 2, width // LANES
    bf16 = jnp.bfloat16
    return pl.pallas_call(
        kernel,
        out_shape=jax.ShapeDtypeStruct((rows, width), jnp.float32),
        in_specs=[pl.BlockSpec(memory_space=pltpu.HBM)] * 2,
        out_specs=pl.BlockSpec(memory_space=pltpu.VMEM),
        scratch_shapes=[
            pltpu.VMEM((count, depth), bf16),
            pltpu.VMEM((2 * count, width), bf16),
            pltpu.VMEM((2, half, 2 * count), bf16),
            pltpu.VMEM((chunks, 16, 3 * rows // 4, LANES), bf16),
            pltpu.VMEM((chunks, 15, 3 * rows // 4, LANES), bf16),
            pltpu.VMEM((chunks // 2, 16, rows // 2, LANES), bf16),
            pltpu.VMEM((chunks // 2, 15, rows // 2, LANES), bf16),
            pltpu.SemaphoreType.DMA((5,)),
            pltpu.SemaphoreType.DMA,
            pltpu.SemaphoreType.DMA((width // WIDE,)),
            pltpu.SemaphoreType.DMA,
            pltpu.SemaphoreType.DMA,
            pltpu.SemaphoreType.DMA,
            pltpu.SemaphoreType.DMA((chunks, 4)),
            pltpu.SemaphoreType.DMA,
            pltpu.SemaphoreType.DMA((chunks // 2, 4)),
        ],
        compiler_params=pltpu.CompilerParams(
            collective_id=0, has_side_effects=True, vmem_limit_bytes=54720 * 1024
        ),
        cost_estimate=pl.CostEstimate(
            flops=2 * count * depth * width,
            bytes_accessed=2 * count * (depth + width) + 4 * rows * width,
            transcendentals=0,
        ),
    )(tokens, cotangent)


def shards(devices, acts, grad_out, inner_weight, first_moment, second_moment, outer_weight, outer_momentum):
    grad = gradient(acts[0], grad_out[0], devices)
    first = 0.9 * first_moment[0] + 0.1 * grad
    second = 0.95 * second_moment[0] + 0.05 * grad * grad
    first_hat = first / (1.0 - 0.9**INNER_STEP)
    second_hat = second / (1.0 - 0.95**INNER_STEP)
    inner_new = inner_weight[0] * (1.0 - 0.0004 * 0.1) - 0.0004 * first_hat / (
        jnp.sqrt(second_hat) + 1e-08
    )
    replicas = lax.axis_size("rep")
    if replicas > 1:
        inner_new = lax.psum_scatter(inner_new, "rep", scatter_dimension=0, tiled=True) / replicas
    pseudo = outer_weight - inner_new
    momentum_next = 0.9 * outer_momentum + pseudo
    outer_next = outer_weight - 0.7 * (pseudo + 0.9 * momentum_next)
    weight_next = outer_next.astype(jnp.bfloat16)
    if replicas > 1:
        weight_next = lax.all_gather(weight_next, "rep", axis=0, tiled=True)
    return (outer_next, momentum_next, weight_next)


def solution(mesh):
    placed = (
        P("rep", "fsdp", None),
        P("rep", "fsdp", None),
        P("rep", "fsdp", None),
        P("rep", "fsdp", None),
        P("rep", "fsdp", None),
        P(("fsdp", "rep"), None),
        P(("fsdp", "rep"), None),
    )
    return jax.shard_map(
        functools.partial(shards, mesh.shape["fsdp"]),
        mesh=mesh,
        in_specs=placed,
        out_specs=(P(("fsdp", "rep"), None), P(("fsdp", "rep"), None), P("fsdp", None)),
        check_vma=False,
    )
```
